512 devices in a mesh: seq: 64 (over y, z), head: 8 (over x, core).
Axes of the slice: x: 4, y: 4, z: 16, core: 2. Of those that a mesh axis runs over, the one named last changes fastest.
Arguments:
- inputs: bfloat16 [16384, 5120], P('seq', 'head'), may hold values from -0.059814453 to 0.059814453
- log_decay: float32 [16384, 80], P('seq', 'head'), may hold values from -0.6 to 0, as said below
- b_proj: bfloat16 [16384, 128], P('seq'), may hold values from -1.796875 to 1.796875
- c_proj: bfloat16 [16384, 128], P('seq'), may hold values from -1.796875 to 1.796875
- grad_out: bfloat16 [16384, 5120], P('seq', 'head'), may hold values from -0.059814453 to 0.059814453
Outputs:
- outputs: bfloat16 [16384, 5120], P('seq', 'head')
- grad_inputs: bfloat16 [16384, 5120], P('seq', 'head')
- grad_log_decay: float32 [16384, 80], P('seq', 'head')
- grad_b: float32 [16384, 128], P('seq')
- grad_c: float32 [16384, 128], P('seq')
The draws below stay inside these ranges and needn't reach their ends.
Inputs may be any that keep to these rules, and one draw needn't show every extreme that they name: log_decay is never positive.
All inputs are finite; a program needn't handle non-finite values.
Results may differ from the reference program's by a relative error of at most 0.01.
Values sent between devices are 32-bit elements; how exact they have to be, the bound alone decides.
A program may use at most 128 MiB of HBM per device.

```python
import math
from functools import partial
import jax
import jax.numpy as jnp
from jax import lax

ATTENDER_COUNT = 80
HEADDIM = 64
STATE = 128
BLOCK = 256
POSITION_TALLY = 16384


def draw_log_decay(key, part):
    generator_seeds = jax.random.split(key, 6)
    slow_share = 5
    slow_heads = jax.random.randint(generator_seeds[0], (ATTENDER_COUNT,), 0, 10) < slow_share
    slow_rate = jax.random.uniform(generator_seeds[1], (ATTENDER_COUNT,), jnp.float32, 0.2, 0.8) / POSITION_TALLY
    fast_rate = jnp.exp(jax.random.uniform(generator_seeds[2], (ATTENDER_COUNT,), jnp.float32, math.log(1.0 / 400.0), math.log(1.0 / 30.0)))
    forgetting_factors = jnp.where(slow_heads, slow_rate, fast_rate)
    rough_approximation = jnp.exp(jax.random.uniform(generator_seeds[3], (POSITION_TALLY, ATTENDER_COUNT), jnp.float32, math.log(0.5), math.log(2.0)))
    input_sequences = jax.random.randint(generator_seeds[4], (POSITION_TALLY, ATTENDER_COUNT), 0, POSITION_TALLY) < 3
    objective_levels = jax.random.uniform(generator_seeds[5], (POSITION_TALLY, ATTENDER_COUNT), jnp.float32, 0.22, 0.51)
    return -(forgetting_factors[None, :] * rough_approximation) - jnp.where(input_sequences, objective_levels, 0.0)


def steps_of(own_key, shape, cuts, smallest, largest):
    def one(position, blocks):
        draws = jax.random.uniform(jax.random.fold_in(jax.random.fold_in(own_key, 6), position), (blocks,), jnp.float32, smallest / len(cuts), largest / len(cuts))
        return jnp.repeat(jnp.exp(draws), shape[position] // blocks).reshape((-1,) + (1,) * (len(shape) - position - 1))

    level = one(*cuts[0])
    for cut in cuts[1:]:
        level = level * one(*cut)
    return level


def centred(rng, shape, scale, limit, cuts=(), held_as=jnp.bfloat16):
    level = steps_of(rng, shape, cuts, -0.22, 0.18) if cuts else 1.0
    values = jax.random.normal(rng, shape, jnp.float32) * scale * level
    return jnp.minimum(jnp.maximum(values, -limit), limit).astype(held_as)


def setup_inputs(seed: int = 0) -> dict:
    keys = jax.random.split(jax.random.key(seed), 6)
    return {
        "inputs": centred(keys[0], (POSITION_TALLY, ATTENDER_COUNT * HEADDIM), 0.01, 0.059814453, ((0, 64), (1, 8))),
        "log_decay": draw_log_decay(jax.random.fold_in(keys[5], 71), 0),
        "b_proj": centred(keys[2], (POSITION_TALLY, STATE), 0.3, 1.796875, ((0, 64),)),
        "c_proj": centred(keys[3], (POSITION_TALLY, STATE), 0.3, 1.796875, ((0, 64),)),
        "grad_out": centred(keys[4], (POSITION_TALLY, ATTENDER_COUNT * HEADDIM), 0.01, 0.059814453, ((0, 64), (1, 8))),
    }


HIGHEST_PRECISION = lax.Precision.HIGHEST

def to_half(values):
    return lax.optimization_barrier(values.astype(jnp.bfloat16)).astype(jnp.float32)

def block_terms(head_signal, head_decay, b_blocks, scores):
    window = head_decay.shape[1]
    causal = jnp.tril(jnp.ones((window, window), dtype=bool))
    prefix = jnp.cumsum(head_decay, axis=1)
    spread = prefix[:, :, None] - prefix[:, None, :]
    decay_mat = jnp.where(causal, jnp.exp(jnp.where(causal, spread, 0.0)), 0.0)
    weighted = to_half(scores * decay_mat)
    within = jnp.einsum('kts,ksp->ktp', weighted, to_half(head_signal), precision=HIGHEST_PRECISION)
    weights = jnp.exp(prefix[:, -1:] - prefix)
    scaled = to_half(head_signal * weights[:, :, None])
    states = jnp.einsum('ksp,ksn->kpn', scaled, to_half(b_blocks), precision=HIGHEST_PRECISION)
    return (prefix, within, states, prefix[:, -1])

def head_terms(pieces, b_blocks, c_blocks, scores):
    head_signal, head_decay = pieces
    prefix, within, states, totals = block_terms(head_signal, head_decay, b_blocks, scores)

    def advance(running, block_pieces):
        block_total, block_state = block_pieces
        return (jnp.exp(block_total) * running + block_state, running)
    final_state, starts = lax.scan(advance, jnp.zeros(states.shape[1:], jnp.float32), (totals, states))
    carried = jnp.einsum('ktn,kpn->ktp', c_blocks, starts, precision=HIGHEST_PRECISION)
    return within + jnp.exp(prefix)[:, :, None] * carried

def score_blocks(b_proj, c_proj):
    blocks = b_proj.shape[0] // BLOCK
    b_half = b_proj.reshape(blocks, BLOCK, STATE)
    c_half = c_proj.reshape(blocks, BLOCK, STATE)
    return jnp.einsum('ktn,ksn->kts', c_half, b_half, preferred_element_type=jnp.float32)

def whole_terms(signal, decays, b_rows, c_rows, scores):
    tokens, head_count = decays.shape
    blocks = tokens // BLOCK
    head_signal = signal.reshape(blocks, BLOCK, head_count, HEADDIM).transpose(2, 0, 1, 3)
    head_decay = decays.reshape(blocks, BLOCK, head_count).transpose(2, 0, 1)
    b_blocks = b_rows.reshape(blocks, BLOCK, STATE)
    c_blocks = c_rows.reshape(blocks, BLOCK, STATE)
    per_head = jax.checkpoint(partial(head_terms, b_blocks=b_blocks, c_blocks=c_blocks, scores=scores))
    outs_heads = lax.map(per_head, (head_signal, head_decay))
    return outs_heads.transpose(1, 2, 0, 3).reshape(tokens, head_count * HEADDIM)

def reference(inputs, log_decay, b_proj, c_proj, grad_out):
    signal = inputs.astype(jnp.float32)
    b_rows = b_proj.astype(jnp.float32)
    c_rows = c_proj.astype(jnp.float32)
    scores = score_blocks(b_proj, c_proj)
    out_f, pull_back = jax.vjp(whole_terms, signal, log_decay, b_rows, c_rows, scores)
    grad_signal, grad_decay, grad_b, grad_c, grad_scores = pull_back(grad_out.astype(jnp.float32))
    blocks = b_rows.shape[0] // BLOCK
    b_blocks = b_rows.reshape(blocks, BLOCK, STATE)
    c_blocks = c_rows.reshape(blocks, BLOCK, STATE)
    half_scores = to_half(grad_scores)
    grad_c = grad_c + jnp.einsum('kts,ksn->ktn', half_scores, b_blocks, precision=HIGHEST_PRECISION).reshape(-1, STATE)
    grad_b = grad_b + jnp.einsum('kts,ktn->ksn', half_scores, c_blocks, precision=HIGHEST_PRECISION).reshape(-1, STATE)
    return (out_f.astype(jnp.bfloat16), grad_signal.astype(jnp.bfloat16), grad_decay, grad_b, grad_c)
```

```python
import functools

import jax
import jax.numpy as jnp
from jax import lax
from jax.experimental import pallas as pl
from jax.experimental.pallas import tpu as pltpu
from jax.sharding import PartitionSpec as P

HEADDIM = 64
STATE = 128
PAIR = 128
HALF = 64
MSG = HALF + 8
GROUP = 4
MESH = pl.DeviceIdType.MESH
F32 = jnp.float32
BF16 = jnp.bfloat16
VMEM = pltpu.MemorySpace.VMEM
HIGHEST = lax.Precision.HIGHEST


def dot(a, b, da=1, db=0, precision=None):
    return lax.dot_general(
        a, b, (((da,), (db,)), ((), ())), precision=precision, preferred_element_type=F32
    )


def split_dot(a, b):
    high = a.astype(BF16)
    low = (a - high.astype(F32)).astype(BF16)
    return dot(high, b) + dot(low, b)


def lower(n, strict=False):
    r = lax.broadcasted_iota(jnp.int32, (n, n), 0)
    c = lax.broadcasted_iota(jnp.int32, (n, n), 1)
    return r > c if strict else r >= c


def head_of_lane(heads, lanes):
    r = lax.broadcasted_iota(jnp.int32, (heads, lanes), 0)
    c = lax.broadcasted_iota(jnp.int32, (heads, lanes), 1)
    return jnp.where(c // HEADDIM == r, 1.0, 0.0).astype(BF16)


def lane_head(lanes, heads):
    r = lax.broadcasted_iota(jnp.int32, (lanes, heads), 0)
    c = lax.broadcasted_iota(jnp.int32, (lanes, heads), 1)
    return jnp.where(r // HEADDIM == c, 1.0, 0.0).astype(BF16)


def decays(ld):
    tokens, heads = ld.shape
    prefix = dot(lower(tokens).astype(F32), ld, precision=HIGHEST)
    spread = head_of_lane(heads, heads * HEADDIM)
    grown = split_dot(jnp.exp(prefix), spread)
    left = split_dot(jnp.exp(prefix[tokens - 1 : tokens] - prefix), spread)
    return prefix, grown, left


def local_kernel(x_ref, ld_ref, b_ref, c_ref, g_ref, sf_ref, sb_ref, within_ref, dxw_ref, gb_ref, gc_ref):
    tokens, heads = ld_ref.shape
    ld = ld_ref[...]
    prefix, grown, left = decays(ld)
    rows = dot(ld, lower(tokens).astype(F32), 0, 1, precision=HIGHEST)
    b, c = b_ref[...], c_ref[...]
    scaled = (x_ref[...].astype(F32) * left).astype(BF16)
    risen = (g_ref[...].astype(F32) * grown).astype(BF16)
    states = dot(b, scaled, 0, 0)
    pulls = dot(c, risen, 0, 0)
    gain = grown[tokens - 1 : tokens]
    for ch in range(heads):
        j, half = ch // 2, ch % 2
        lanes = slice(j * PAIR, (j + 1) * PAIR)
        span = slice(half * HALF, (half + 1) * HALF)
        tile = jnp.broadcast_to(gain[:, lanes], (8, PAIR))
        sf_ref[ch, :HALF] = states[span, lanes]
        sf_ref[ch, HALF:] = tile
        sb_ref[ch, :HALF] = pulls[span, lanes]
        sb_ref[ch, HALF:] = tile
    scores = dot(c, b, 1, 1)
    causal = lower(tokens)
    first = lax.broadcasted_iota(jnp.int32, (tokens, PAIR), 1) < HEADDIM
    total = jnp.zeros((tokens, tokens), F32)
    for j in range(heads // 2):
        lanes = slice(j * PAIR, (j + 1) * PAIR)
        xp, gp = x_ref[:, lanes], g_ref[:, lanes]
        parts = []
        for e in range(2):
            h = 2 * j + e
            decay = jnp.where(causal, jnp.exp(prefix[:, h : h + 1] - rows[h : h + 1]), 0.0)
            weighted = (scores * decay).astype(BF16)
            own = jnp.where(first if e == 0 else ~first, gp.astype(F32), 0.0).astype(BF16)
            total += dot(own, xp, 1, 1) * decay
            parts.append((dot(weighted, xp), dot(weighted, gp, 0, 0)))
        within_ref[:, lanes] = jnp.where(first, parts[0][0], parts[1][0])
        dxw_ref[:, lanes] = jnp.where(first, parts[0][1], parts[1][1])
    halved = total.astype(BF16)
    gc_ref[...] = dot(halved, b)
    gb_ref[...] = dot(halved, c, 0, 0)


def after_kernel(
    x_ref, ld_ref, b_ref, c_ref, g_ref, within_ref, dxw_ref, gb_ref, gc_ref, start_ref, adj_ref,
    out_ref, dx_ref, dld_ref, both_ref,
):
    tokens, heads = ld_ref.shape
    prefix, grown, left = decays(ld_ref[...])
    b, c = b_ref[...], c_ref[...]
    gain = grown[tokens - 1 : tokens]
    spread = lane_head(heads * HEADDIM, heads)
    gb, gc = gb_ref[...], gc_ref[...]
    rising = jnp.zeros((tokens, heads), F32)
    falling = jnp.zeros((tokens, heads), F32)
    last = jnp.zeros((8, heads), F32)
    for j in range(heads // 2):
        lanes = slice(j * PAIR, (j + 1) * PAIR)
        x, g = x_ref[:, lanes].astype(F32), g_ref[:, lanes].astype(F32)
        start = jnp.concatenate([start_ref[2 * j], start_ref[2 * j + 1]], axis=0)
        adj = jnp.concatenate([adj_ref[2 * j], adj_ref[2 * j + 1]], axis=0)
        start16, adj16 = start.astype(BF16), adj.astype(BF16)
        own = spread[lanes]
        out = within_ref[:, lanes] + grown[:, lanes] * dot(c, start16)
        pushed = left[:, lanes] * dot(b, adj16)
        out_ref[:, lanes] = out.astype(BF16)
        dx_ref[:, lanes] = (dxw_ref[:, lanes] + pushed).astype(BF16)
        gc += dot((g * grown[:, lanes]).astype(BF16), start16, 1, 1)
        gb += dot((x * left[:, lanes]).astype(BF16), adj16, 1, 1)
        rising += split_dot(g * out - x * dxw_ref[:, lanes], own)
        falling += split_dot(x * pushed, own)
        meet = jnp.sum(start * adj, axis=0, keepdims=True) * gain[:, lanes]
        last += split_dot(jnp.broadcast_to(meet, (8, PAIR)), own)
    dld_ref[...] = (
        dot(lower(tokens).astype(F32), rising, 0, 0, precision=HIGHEST)
        + dot(lower(tokens, True).astype(F32), falling, precision=HIGHEST)
        + last[:1]
    )
    both_ref[:tokens] = gb
    both_ref[tokens:] = gc


def carry_kernel(
    sf_ref, sb_ref, start_ref, adj_ref,
    own_in, up_in, up_out, at_owner, from_owner, down_in, down_out,
    up_send, up_recv, own_recv, own_send, down_recv, down_send, rep_send,
):
    chunks = sf_ref.shape[0]
    groups = lax.axis_size("seq") // GROUP
    seq, head = lax.axis_index("seq"), lax.axis_index("head")
    group, place = seq // GROUP, lax.rem(seq, GROUP)
    shift = lax.rem(head, 2) * chunks
    outer = (place == 0) | (place == GROUP - 1)
    early = jnp.where(place < GROUP // 2, 0, 1)
    late = 1 - early
    ahead = jnp.where(early == 0, 1, -1)

    def owner(scan, ch):
        where = lax.rem(ch + shift, groups)
        return (jnp.where(scan == 0, where * GROUP + 1, (groups - 1 - where) * GROUP + 2), head)

    mine = lax.rem(group - shift + 2 * groups, groups)
    mine = jnp.where(place == 1, mine, lax.rem(groups - 1 - group - shift + 2 * groups, groups))
    owns = ~outer & (mine < chunks)
    scan_owned = place - 1

    barrier = pltpu.get_barrier_semaphore()

    def greet(where):
        pl.semaphore_signal(barrier, inc=1, device_id=where, device_id_type=MESH)

    @pl.when(outer)
    def _():
        greet((seq + ahead, head))

        def both(ch, _):
            greet(owner(0, ch))
            greet(owner(1, ch))
            return 0

        lax.fori_loop(0, chunks, both, 0)
        pl.semaphore_wait(barrier, 2 * chunks + 1)

    @pl.when(~outer)
    def _():
        greet((seq + 1, head))
        greet((seq - 1, head))

        @pl.when(owns)
        def _():
            def each(k, _):
                greet((k * GROUP, head))
                greet((k * GROUP + GROUP - 1, head))
                return 0

            lax.fori_loop(0, groups, each, 0)
            pl.semaphore_wait(barrier, 2 * groups + 2)

        @pl.when(~owns)
        def _():
            pl.semaphore_wait(barrier, 2)

    own_in[0] = sf_ref[...]
    own_in[1] = sb_ref[...]

    def up_copy(scan, ch, source, to):
        return pltpu.make_async_remote_copy(
            src_ref=source, dst_ref=up_in.at[scan, ch], send_sem=up_send.at[scan, ch],
            recv_sem=up_recv.at[scan, ch], device_id=to, device_id_type=MESH,
        )

    def down_copy(scan, ch, to):
        return pltpu.make_async_remote_copy(
            src_ref=down_out.at[scan, ch], dst_ref=down_in.at[scan, ch], send_sem=down_send.at[scan, ch],
            recv_sem=down_recv.at[scan, ch], device_id=to, device_id_type=MESH,
        )

    def owner_copy(scan, ch):
        k = jnp.where(scan == 0, group, groups - 1 - group)
        return pltpu.make_async_remote_copy(
            src_ref=up_out.at[scan, ch], dst_ref=at_owner.at[k], send_sem=rep_send.at[ch],
            recv_sem=own_recv.at[k], device_id=owner(scan, ch), device_id_type=MESH,
        )

    def back_copy(k):
        to = jnp.where(scan_owned == 0, k * GROUP, (groups - 1 - k) * GROUP + GROUP - 1)
        return pltpu.make_async_remote_copy(
            src_ref=from_owner.at[k], dst_ref=down_in.at[scan_owned, mine], send_sem=own_send.at[k],
            recv_sem=down_recv.at[scan_owned, mine], device_id=(to, head), device_id_type=MESH,
        )

    e_to, l_to = (seq + ahead, head), (seq - ahead, head)

    def rise(scan, ch):
        gain = own_in[scan, ch, HALF:]
        carried = up_in[scan, ch, HALF:]
        up_out[scan, ch, :HALF] = own_in[scan, ch, :HALF] + gain[:1] * up_in[scan, ch, :HALF]
        up_out[scan, ch, HALF:] = gain * carried

    def up_wait(scan, ch):
        up_copy(scan, ch, up_out.at[scan, ch], e_to).wait_recv()

    @pl.when(outer)
    def _():
        def send(ch, _):
            up_copy(early, ch, own_in.at[early, ch], e_to).start()
            return 0

        lax.fori_loop(0, chunks, send, 0)

        def total(ch, _):
            up_wait(late, ch)
            rise(late, ch)
            owner_copy(late, ch).start()
            return 0

        lax.fori_loop(0, chunks, total, 0)

    lag = min(4, chunks)

    @pl.when(~outer)
    def _():
        def step(i, _):
            @pl.when(i < chunks)
            def _():
                up_wait(early, i)
                rise(early, i)
                up_copy(early, i, up_out.at[early, i], e_to).start()

            @pl.when(i >= lag)
            def _():
                ch = i - lag
                up_wait(late, ch)
                rise(late, ch)
                up_copy(late, ch, up_out.at[late, ch], l_to).start()

            return 0

        lax.fori_loop(0, chunks + lag, step, 0)

    @pl.when(owns)
    def _():
        def scan_groups(k, carry):
            from_owner[k] = carry
            back_copy(k).start()
            pltpu.make_async_remote_copy(
                src_ref=at_owner.at[k], dst_ref=at_owner.at[k], send_sem=own_send.at[k],
                recv_sem=own_recv.at[k], device_id=(seq + 1, head), device_id_type=MESH,
            ).wait_recv()
            return at_owner[k, HALF : HALF + 1] * carry + at_owner[k, :HALF]

        lax.fori_loop(0, groups, scan_groups, jnp.zeros((HALF, PAIR), F32))

    def down_wait(scan, ch):
        down_copy(scan, ch, e_to).wait_recv()

    def fall(scan, ch):
        down_out[scan, ch] = (
            own_in[scan, ch, :HALF] + own_in[scan, ch, HALF : HALF + 1] * down_in[scan, ch]
        )

    @pl.when(outer)
    def _():
        def step(i, _):
            @pl.when(i < chunks)
            def _():
                down_wait(early, i)
                fall(early, i)
                down_copy(early, i, e_to).start()

            return 0

        lax.fori_loop(0, chunks, step, 0)

        def end(ch, _):
            down_wait(late, ch)
            return 0

        lax.fori_loop(0, chunks, end, 0)

    @pl.when(~outer)
    def _():
        def step(i, _):
            @pl.when(i < chunks)
            def _():
                down_wait(early, i)
                fall(early, i)
                down_copy(early, i, e_to).start()

            @pl.when(i >= lag)
            def _():
                ch = i - lag
                down_wait(late, ch)
                fall(late, ch)
                down_copy(late, ch, l_to).start()

            return 0

        lax.fori_loop(0, chunks + lag, step, 0)

    start_ref[...] = down_in[0]
    adj_ref[...] = down_in[1]

    def left(ch, _):
        up_copy(early, ch, up_out.at[early, ch], e_to).wait_send()
        down_copy(early, ch, e_to).wait_send()

        @pl.when(outer)
        def _():
            owner_copy(late, ch).wait_send()

        @pl.when(~outer)
        def _():
            up_copy(late, ch, up_out.at[late, ch], l_to).wait_send()
            down_copy(late, ch, l_to).wait_send()

        return 0

    lax.fori_loop(0, chunks, left, 0)

    @pl.when(owns)
    def _():
        def sent(k, _):
            back_copy(k).wait_send()
            return 0

        lax.fori_loop(0, groups, sent, 0)


def carry(sf, sb):
    chunks = sf.shape[0]
    groups = lax.axis_size("seq") // GROUP
    state = jax.ShapeDtypeStruct((chunks, HALF, PAIR), F32)
    dma = pltpu.SemaphoreType.DMA
    return pl.pallas_call(
        carry_kernel,
        out_shape=(state, state),
        in_specs=[pl.BlockSpec(memory_space=VMEM)] * 2,
        out_specs=(pl.BlockSpec(memory_space=VMEM),) * 2,
        scratch_shapes=[
            pltpu.VMEM((2, chunks, MSG, PAIR), F32),
            pltpu.VMEM((2, chunks, MSG, PAIR), F32),
            pltpu.VMEM((2, chunks, MSG, PAIR), F32),
            pltpu.VMEM((groups, MSG, PAIR), F32),
            pltpu.VMEM((groups, HALF, PAIR), F32),
            pltpu.VMEM((2, chunks, HALF, PAIR), F32),
            pltpu.VMEM((2, chunks, HALF, PAIR), F32),
            dma((2, chunks)), dma((2, chunks)), dma((groups,)), dma((groups,)),
            dma((2, chunks)), dma((2, chunks)), dma((chunks,)),
        ],
        compiler_params=pltpu.CompilerParams(
            collective_id=0, has_side_effects=True, vmem_limit_bytes=48 * 2**20
        ),
        name="carry",
    )(sf, sb)


def sum_kernel(n, both_ref, sum_ref, parts, done, part_send, part_recv, done_send, done_recv):
    seq, head = lax.axis_index("seq"), lax.axis_index("head")
    rows = both_ref.shape[0] // n
    barrier = pltpu.get_barrier_semaphore()
    for step in range(1, n):
        pl.semaphore_signal(
            barrier, inc=1, device_id=(seq, lax.rem(head + step, n)), device_id_type=MESH
        )
    pl.semaphore_wait(barrier, n - 1)

    def part(step):
        to = lax.rem(head + step, n)
        return pltpu.make_async_remote_copy(
            src_ref=both_ref.at[pl.ds(pl.multiple_of(to * rows, rows), rows)], dst_ref=parts.at[step],
            send_sem=part_send.at[step], recv_sem=part_recv.at[step],
            device_id=(seq, to), device_id_type=MESH,
        )

    def whole(step):
        to = lax.rem(head + step, n)
        here = pl.ds(pl.multiple_of(head * rows, rows), rows)
        return pltpu.make_async_remote_copy(
            src_ref=done.at[here], dst_ref=done.at[here], send_sem=done_send.at[step],
            recv_sem=done_recv.at[step], device_id=(seq, to), device_id_type=MESH,
        )

    for step in range(1, n):
        part(step).start()
    here = pl.ds(pl.multiple_of(head * rows, rows), rows)
    total = both_ref[here]
    for step in range(1, n):
        part(step).wait_recv()
        total += parts[step]
    done[here] = total
    for step in range(1, n):
        whole(step).start()
    for step in range(1, n):
        part(step).wait_send()
    for step in range(1, n):
        whole(step).wait()
    sum_ref[...] = done[...]


def summed(both):
    n = lax.axis_size("head")
    rows, columns = both.shape
    dma = pltpu.SemaphoreType.DMA
    return pl.pallas_call(
        functools.partial(sum_kernel, n),
        out_shape=jax.ShapeDtypeStruct(both.shape, F32),
        in_specs=[pl.BlockSpec(memory_space=VMEM)],
        out_specs=pl.BlockSpec(memory_space=VMEM),
        scratch_shapes=[
            pltpu.VMEM((n, rows // n, columns), F32),
            pltpu.VMEM((rows, columns), F32),
            dma((n,)), dma((n,)), dma((n,)), dma((n,)),
        ],
        compiler_params=pltpu.CompilerParams(collective_id=1, has_side_effects=True),
        name="summed",
    )(both)


def shards(inputs, log_decay, b_proj, c_proj, grad_out):
    tokens, heads = log_decay.shape
    wide = jax.ShapeDtypeStruct(inputs.shape, F32)
    thin = jax.ShapeDtypeStruct((tokens, STATE), F32)
    message = jax.ShapeDtypeStruct((heads, MSG, PAIR), F32)
    whole = pl.BlockSpec(memory_space=VMEM)
    room = pltpu.CompilerParams(vmem_limit_bytes=48 * 2**20)
    sf, sb, within, dxw, gb, gc = pl.pallas_call(
        local_kernel,
        out_shape=(message, message, wide, wide, thin, thin),
        in_specs=[whole] * 5, out_specs=(whole,) * 6, compiler_params=room, name="local",
    )(inputs, log_decay, b_proj, c_proj, grad_out)
    start, adj = carry(sf, sb)
    outputs, grad_inputs, grad_decay, both = pl.pallas_call(
        after_kernel,
        out_shape=(
            jax.ShapeDtypeStruct(inputs.shape, BF16),
            jax.ShapeDtypeStruct(inputs.shape, BF16),
            jax.ShapeDtypeStruct(log_decay.shape, F32),
            jax.ShapeDtypeStruct((2 * tokens, STATE), F32),
        ),
        in_specs=[whole] * 11, out_specs=(whole,) * 4, compiler_params=room, name="after",
    )(inputs, log_decay, b_proj, c_proj, grad_out, within, dxw, gb, gc, start, adj)
    both = summed(both)
    return outputs, grad_inputs, grad_decay, both[:tokens], both[tokens:]


def solution(mesh):
    placed = (P("seq", "head"), P("seq", "head"), P("seq", None), P("seq", None), P("seq", "head"))
    return jax.shard_map(
        shards,
        mesh=mesh,
        in_specs=placed,
        out_specs=(
            P("seq", "head"),
            P("seq", "head"),
            P("seq", "head"),
            P("seq", None),
            P("seq", None),
        ),
        check_vma=False,
    )
```

```python
import jax
import jax.numpy as jnp
from jax import lax
from jax.experimental import pallas as pl
from jax.experimental.pallas import tpu as pltpu
from jax.sharding import PartitionSpec as P

HEADDIM = 64
STATE = 128
PAIR = 128
GROUP = 4
LAG = 5
MESH = pl.DeviceIdType.MESH
F32 = jnp.float32
BF16 = jnp.bfloat16
VMEM = pltpu.MemorySpace.VMEM
HIGHEST = lax.Precision.HIGHEST


def dot(a, b, da=1, db=0, precision=None):
    return lax.dot_general(
        a, b, (((da,), (db,)), ((), ())), precision=precision, preferred_element_type=F32
    )


def split_dot(a, b):
    high = a.astype(BF16)
    low = (a - high.astype(F32)).astype(BF16)
    return dot(high, b) + dot(low, b)


def lower(n, strict=False):
    r = lax.broadcasted_iota(jnp.int32, (n, n), 0)
    c = lax.broadcasted_iota(jnp.int32, (n, n), 1)
    return r > c if strict else r >= c


def head_of_lane(heads, lanes):
    r = lax.broadcasted_iota(jnp.int32, (heads, lanes), 0)
    c = lax.broadcasted_iota(jnp.int32, (heads, lanes), 1)
    return jnp.where(c // HEADDIM == r, 1.0, 0.0).astype(BF16)


def lane_head(lanes, heads):
    r = lax.broadcasted_iota(jnp.int32, (lanes, heads), 0)
    c = lax.broadcasted_iota(jnp.int32, (lanes, heads), 1)
    return jnp.where(r // HEADDIM == c, 1.0, 0.0).astype(BF16)


def decays(ldt):
    heads, tokens = ldt.shape
    prefix = dot(lower(tokens).astype(F32), ldt, 1, 1, precision=HIGHEST)
    spread = head_of_lane(heads, heads * HEADDIM)
    grown = split_dot(jnp.exp(prefix), spread)
    left = split_dot(jnp.exp(prefix[tokens - 1 : tokens] - prefix), spread)
    return prefix, grown, left


def main_kernel(
    x_ref, ldt_ref, b_ref, c_ref, g_ref, out_ref, dx_ref, dldt_ref, gb_ref, gc_ref,
    grown_ref, left_ref, within_ref, dxw_ref, factor, grads,
    own_in, up_in, up_out, down_in, down_out, at_owner, from_owner,
    gain_own, gain_in, gain_out, gain_at, unit_out, unit_in, full,
    up_send, up_recv, own_recv, own_send, down_recv, down_send, rep_send,
    gain_send, gain_recv, gain_far_send, gain_far_recv, unit_send, unit_recv, full_send, full_recv,
):
    heads, tokens = ldt_ref.shape
    lanes = heads * HEADDIM
    pairs = lanes // PAIR
    groups = lax.axis_size("seq") // GROUP
    peers = lax.axis_size("head")
    chunks = groups
    deep = STATE // chunks
    parts = peers // 2
    per = chunks // parts
    wide = STATE // parts
    seq, head = lax.axis_index("seq"), lax.axis_index("head")
    group, place = seq // GROUP, lax.rem(seq, GROUP)
    shift = lax.rem(head, 2) * (groups // 2)
    outer = (place == 0) | (place == GROUP - 1)
    early = jnp.where(place < GROUP // 2, 0, 1)
    late = 1 - early
    ahead = jnp.where(early == 0, 1, -1)
    e_to, l_to = (seq + ahead, head), (seq - ahead, head)

    def owner(scan, ch):
        where = lax.rem(ch + shift, groups)
        return (jnp.where(scan == 0, where * GROUP + 1, (groups - 1 - where) * GROUP + 2), head)

    scan_owned = jnp.where(place == 1, 0, 1)
    mine = lax.rem(jnp.where(place == 1, group, groups - 1 - group) + groups - shift, groups)

    barrier = pltpu.get_barrier_semaphore()

    def greet(where):
        pl.semaphore_signal(barrier, inc=1, device_id=where, device_id_type=MESH)

    @pl.when(outer)
    def _():
        def each(k, _):
            greet((k * GROUP + 1, head))
            greet((k * GROUP + 2, head))
            return 0

        lax.fori_loop(0, groups, each, 0)

    @pl.when(~outer)
    def _():
        def each(k, _):
            greet((k * GROUP, head))
            greet((k * GROUP + GROUP - 1, head))
            return 0

        lax.fori_loop(0, groups, each, 0)
        greet((jnp.where(place == 1, seq + 1, seq - 1), head))

    for step in range(1, peers):
        greet((seq, lax.rem(head + step, peers)))

    ldt = ldt_ref[...]
    prefix, grown, left = decays(ldt)
    grown_ref[...] = grown
    left_ref[...] = left
    rows = dot(ldt, lower(tokens).astype(F32), 1, 1, precision=HIGHEST)
    b, c = b_ref[...], c_ref[...]
    risen = (g_ref[...].astype(F32) * grown).astype(BF16)
    scaled = (x_ref[...].astype(F32) * left).astype(BF16)
    factor[0] = risen
    factor[1] = scaled
    own_in[0] = dot(b, scaled, 0, 0).reshape(chunks, deep, lanes)
    own_in[1] = dot(c, risen, 0, 0).reshape(chunks, deep, lanes)
    for j in range(pairs):
        gain_own[j : j + 1] = grown[tokens - 1 : tokens, j * PAIR : (j + 1) * PAIR]
    gain_own[pairs:] = jnp.zeros((8 - pairs, PAIR), F32)

    scores = dot(c, b, 1, 1)
    causal = lower(tokens)
    first = lax.broadcasted_iota(jnp.int32, (tokens, PAIR), 1) < HEADDIM
    total = jnp.zeros((tokens, tokens), F32)
    for j in range(pairs):
        span = slice(j * PAIR, (j + 1) * PAIR)
        xp, gp = x_ref[:, span], g_ref[:, span]
        found = []
        for e in range(2):
            h = 2 * j + e
            decay = jnp.where(causal, jnp.exp(prefix[:, h : h + 1] - rows[h : h + 1]), 0.0)
            weighted = (scores * decay).astype(BF16)
            own = jnp.where(first if e == 0 else ~first, gp.astype(F32), 0.0).astype(BF16)
            total += dot(own, xp, 1, 1) * decay
            found.append((dot(weighted, xp), dot(weighted, gp, 0, 0)))
        within_ref[:, span] = jnp.where(first, found[0][0], found[1][0])
        dxw_ref[:, span] = jnp.where(first, found[0][1], found[1][1])
    halved = total.astype(BF16)
    grads[0] = dot(b, halved, 0, 1)
    grads[1] = dot(c, halved, 0, 0)

    @pl.when(outer)
    def _():
        pl.semaphore_wait(barrier, 2 * groups + peers - 1)

    @pl.when(~outer)
    def _():
        pl.semaphore_wait(barrier, 2 * groups + 1 + peers - 1)

    def up_copy(scan, ch, source, to):
        return pltpu.make_async_remote_copy(
            src_ref=source, dst_ref=up_in.at[scan, ch], send_sem=up_send.at[scan, ch],
            recv_sem=up_recv.at[scan, ch], device_id=to, device_id_type=MESH,
        )

    def gain_copy(scan, source, to):
        return pltpu.make_async_remote_copy(
            src_ref=source, dst_ref=gain_in.at[scan], send_sem=gain_send.at[scan],
            recv_sem=gain_recv.at[scan], device_id=to, device_id_type=MESH,
        )

    def down_copy(scan, ch, to):
        return pltpu.make_async_remote_copy(
            src_ref=down_out.at[scan, ch], dst_ref=down_in.at[scan, ch], send_sem=down_send.at[scan, ch],
            recv_sem=down_recv.at[scan, ch], device_id=to, device_id_type=MESH,
        )

    rank = jnp.where(late == 0, group, groups - 1 - group)

    def owner_copy(ch):
        return pltpu.make_async_remote_copy(
            src_ref=up_out.at[late, ch], dst_ref=at_owner.at[rank], send_sem=rep_send.at[ch],
            recv_sem=own_recv.at[rank], device_id=owner(late, ch), device_id_type=MESH,
        )

    def gain_far_copy(ch):
        return pltpu.make_async_remote_copy(
            src_ref=gain_out.at[late], dst_ref=gain_at.at[rank], send_sem=gain_far_send.at[ch],
            recv_sem=gain_far_recv.at[rank], device_id=owner(late, ch), device_id_type=MESH,
        )

    def arrived(buffer, sem, k):
        pltpu.make_async_remote_copy(
            src_ref=buffer.at[k], dst_ref=buffer.at[k], send_sem=own_send.at[k],
            recv_sem=sem.at[k], device_id=e_to, device_id_type=MESH,
        ).wait_recv()

    def back_copy(k):
        to = jnp.where(scan_owned == 0, k * GROUP, (groups - 1 - k) * GROUP + GROUP - 1)
        return pltpu.make_async_remote_copy(
            src_ref=from_owner.at[k], dst_ref=down_in.at[scan_owned, mine], send_sem=own_send.at[k],
            recv_sem=down_recv.at[scan_owned, mine], device_id=(to, head), device_id_type=MESH,
        )

    def unit_copy(u):
        return pltpu.make_async_remote_copy(
            src_ref=unit_out.at[u], dst_ref=unit_in.at[head], send_sem=unit_send.at[u],
            recv_sem=unit_recv.at[head], device_id=(seq, u), device_id_type=MESH,
        )

    def unit_from(u):
        return pltpu.make_async_remote_copy(
            src_ref=unit_in.at[u], dst_ref=unit_in.at[u], send_sem=unit_send.at[u],
            recv_sem=unit_recv.at[u], device_id=(seq, u), device_id_type=MESH,
        )

    def full_copy(u):
        return pltpu.make_async_remote_copy(
            src_ref=full.at[head], dst_ref=full.at[head], send_sem=full_send.at[u],
            recv_sem=full_recv.at[head], device_id=(seq, u), device_id_type=MESH,
        )

    def full_from(u):
        return pltpu.make_async_remote_copy(
            src_ref=full.at[u], dst_ref=full.at[u], send_sem=full_send.at[u],
            recv_sem=full_recv.at[u], device_id=(seq, u), device_id_type=MESH,
        )

    gain = jnp.concatenate([gain_own[j : j + 1] for j in range(pairs)], axis=1)

    def rise(scan, ch):
        up_copy(scan, ch, up_out.at[scan, ch], e_to).wait_recv()
        up_out[scan, ch] = own_in[scan, ch] + gain * up_in[scan, ch]

    def gain_rise(scan):
        gain_copy(scan, gain_own, e_to).wait_recv()
        gain_out[scan] = gain_own[...] * gain_in[scan]

    @pl.when(outer)
    def _():
        gain_copy(early, gain_own, e_to).start()

        def send(ch, _):
            up_copy(early, ch, own_in.at[early, ch], e_to).start()
            return 0

        lax.fori_loop(0, chunks, send, 0)
        gain_rise(late)

        def tell(ch, _):
            gain_far_copy(ch).start()
            return 0

        lax.fori_loop(0, chunks, tell, 0)

        def finish(ch, _):
            rise(late, ch)
            owner_copy(ch).start()
            return 0

        lax.fori_loop(0, chunks, finish, 0)

    lag = min(LAG, chunks)

    @pl.when(~outer)
    def _():
        gain_rise(early)
        gain_copy(early, gain_out.at[early], e_to).start()

        def step(i, _):
            @pl.when(i < chunks)
            def _():
                rise(early, i)
                up_copy(early, i, up_out.at[early, i], e_to).start()

            @pl.when(i == lag)
            def _():
                gain_rise(late)
                gain_copy(late, gain_out.at[late], l_to).start()

            @pl.when(i >= lag)
            def _():
                rise(late, i - lag)
                up_copy(late, i - lag, up_out.at[late, i - lag], l_to).start()

            return 0

        lax.fori_loop(0, chunks + lag, step, 0)

        def hand_out(k, entering):
            from_owner[k] = entering
            back_copy(k).start()
            arrived(gain_at, gain_far_recv, k)
            arrived(at_owner, own_recv, k)
            gains = jnp.concatenate([gain_at[k, j : j + 1] for j in range(pairs)], axis=1)
            return gains * entering + at_owner[k]

        lax.fori_loop(0, groups, hand_out, jnp.zeros((deep, lanes), F32))

    def landed(scan, ch):
        down_copy(scan, ch, e_to).wait_recv()

    def fall(scan, ch, to):
        landed(scan, ch)
        down_out[scan, ch] = own_in[scan, ch] + gain * down_in[scan, ch]
        down_copy(scan, ch, to).start()

    def unit(scan, ch):
        @pl.when(lax.rem(ch + 1, per) == 0)
        def _():
            q = ch // per
            u = scan * parts + q
            state = down_in[scan, pl.ds(q * per, per)].reshape(wide, lanes).astype(BF16)
            part = grads[scan, pl.ds(pl.multiple_of(q * wide, wide), wide)]
            unit_out[u] = part + dot(state, factor[scan], 1, 1)

            @pl.when(u != head)
            def _():
                unit_copy(u).start()

    @pl.when(outer)
    def _():
        def one(i, _):
            fall(early, i, e_to)
            unit(early, i)
            return 0

        lax.fori_loop(0, chunks, one, 0)

        def two(i, _):
            landed(late, i)
            unit(late, i)
            return 0

        lax.fori_loop(0, chunks, two, 0)

    @pl.when(~outer)
    def _():
        def step(i, _):
            @pl.when(i < chunks)
            def _():
                fall(early, i, e_to)

            @pl.when(i >= lag)
            def _():
                fall(late, i - lag, l_to)

            @pl.when(i < chunks)
            def _():
                unit(early, i)

            @pl.when(i >= lag)
            def _():
                unit(late, i - lag)

            return 0

        lax.fori_loop(0, chunks + lag, step, 0)

    spread = lane_head(lanes, heads)
    rising = jnp.zeros((tokens, heads), F32)
    falling = jnp.zeros((tokens, heads), F32)
    start = down_in[0].reshape(STATE, lanes)
    adj = down_in[1].reshape(STATE, lanes)
    for j in range(pairs):
        span = slice(j * PAIR, (j + 1) * PAIR)
        x, g = x_ref[:, span].astype(F32), g_ref[:, span].astype(F32)
        own = spread[span]
        out = within_ref[:, span] + grown_ref[:, span] * dot(c, start[:, span].astype(BF16))
        pushed = left_ref[:, span] * dot(b, adj[:, span].astype(BF16))
        out_ref[:, span] = out.astype(BF16)
        dx_ref[:, span] = (dxw_ref[:, span] + pushed).astype(BF16)
        rising += split_dot(g * out - x * dxw_ref[:, span], own)
        falling += split_dot(x * pushed, own)

    def add(o, total):
        u = lax.rem(head + o, peers)
        unit_from(u).wait_recv()
        return total + unit_in[u]

    full[head] = lax.fori_loop(1, peers, add, unit_out[head])
    for o in range(1, peers):
        full_copy(lax.rem(head + o, peers)).start()

    meet = jnp.sum(start * adj, axis=0, keepdims=True) * gain
    meet = jnp.broadcast_to(meet, (8, lanes))
    high = meet.astype(BF16)
    low = (meet - high.astype(F32)).astype(BF16)
    where = head_of_lane(heads, lanes)
    last = dot(where, high, 1, 1) + dot(where, low, 1, 1)
    dldt_ref[...] = (
        dot(rising, lower(tokens).astype(F32), 0, 0, precision=HIGHEST)
        + dot(falling, lower(tokens, True).astype(F32), 0, 1, precision=HIGHEST)
        + last[:, :1]
    )

    gain_copy(early, gain_own, e_to).wait_send()

    def gone(ch, _):
        up_copy(early, ch, up_out.at[early, ch], e_to).wait_send()
        down_copy(early, ch, e_to).wait_send()

        @pl.when(outer)
        def _():
            owner_copy(ch).wait_send()
            gain_far_copy(ch).wait_send()

        @pl.when(~outer)
        def _():
            up_copy(late, ch, up_out.at[late, ch], l_to).wait_send()
            down_copy(late, ch, l_to).wait_send()
            back_copy(ch).wait_send()

        return 0

    lax.fori_loop(0, chunks, gone, 0)

    @pl.when(~outer)
    def _():
        gain_copy(late, gain_own, l_to).wait_send()

    for o in range(1, peers):
        u = lax.rem(head + o, peers)
        unit_copy(u).wait_send()
        full_copy(u).wait_send()
        full_from(u).wait_recv()
    gc_ref[...] = full[:parts].reshape(STATE, tokens).T
    gb_ref[...] = full[parts:].reshape(STATE, tokens).T


def shards(inputs, log_decay, b_proj, c_proj, grad_out):
    tokens, heads = log_decay.shape
    lanes = heads * HEADDIM
    groups = lax.axis_size("seq") // GROUP
    peers = lax.axis_size("head")
    deep = STATE // groups
    unit = (peers, STATE // (peers // 2), tokens)
    chunk = (2, groups, deep, lanes)
    dma = pltpu.SemaphoreType.DMA
    half = jax.ShapeDtypeStruct(inputs.shape, BF16)
    thin = jax.ShapeDtypeStruct((tokens, STATE), F32)
    whole = pl.BlockSpec(memory_space=VMEM)
    outputs, grad_inputs, grad_decay, grad_b, grad_c = pl.pallas_call(
        main_kernel,
        out_shape=(half, half, jax.ShapeDtypeStruct((heads, tokens), F32), thin, thin),
        in_specs=[whole] * 5,
        out_specs=(whole,) * 5,
        scratch_shapes=[
            pltpu.VMEM((tokens, lanes), F32), pltpu.VMEM((tokens, lanes), F32),
            pltpu.VMEM((tokens, lanes), F32), pltpu.VMEM((tokens, lanes), F32),
            pltpu.VMEM((2, tokens, lanes), BF16), pltpu.VMEM((2, STATE, tokens), F32),
            pltpu.VMEM(chunk, F32), pltpu.VMEM(chunk, F32), pltpu.VMEM(chunk, F32),
            pltpu.VMEM(chunk, F32), pltpu.VMEM(chunk, F32),
            pltpu.VMEM((groups, deep, lanes), F32), pltpu.VMEM((groups, deep, lanes), F32),
            pltpu.VMEM((8, PAIR), F32), pltpu.VMEM((2, 8, PAIR), F32), pltpu.VMEM((2, 8, PAIR), F32),
            pltpu.VMEM((groups, 8, PAIR), F32),
            pltpu.VMEM(unit, F32), pltpu.VMEM(unit, F32), pltpu.VMEM(unit, F32),
            dma((2, groups)), dma((2, groups)), dma((groups,)), dma((groups,)),
            dma((2, groups)), dma((2, groups)), dma((groups,)),
            dma((2,)), dma((2,)), dma((groups,)), dma((groups,)),
            dma((peers,)), dma((peers,)), dma((peers,)), dma((peers,)),
        ],
        compiler_params=pltpu.CompilerParams(
            collective_id=0, has_side_effects=True, vmem_limit_bytes=56 * 2**20
        ),
        name="scan",
    )(inputs, log_decay.T, b_proj, c_proj, grad_out)
    return outputs, grad_inputs, grad_decay.T, grad_b, grad_c


def solution(mesh):
    placed = (P("seq", "head"), P("seq", "head"), P("seq", None), P("seq", None), P("seq", "head"))
    return jax.shard_map(
        shards,
        mesh=mesh,
        in_specs=placed,
        out_specs=(
            P("seq", "head"),
            P("seq", "head"),
            P("seq", "head"),
            P("seq", None),
            P("seq", None),
        ),
        check_vma=False,
    )
```

```python
import jax
import jax.numpy as jnp
from jax import lax
from jax.experimental import pallas as pl
from jax.experimental.pallas import tpu as pltpu
from jax.sharding import PartitionSpec as P

HEADDIM = 64
STATE = 128
PAIR = 128
GROUP = 4
LAG = 5
MESH = pl.DeviceIdType.MESH
F32 = jnp.float32
BF16 = jnp.bfloat16
VMEM = pltpu.MemorySpace.VMEM
HIGHEST = lax.Precision.HIGHEST


def dot(a, b, da=1, db=0, precision=None):
    return lax.dot_general(
        a, b, (((da,), (db,)), ((), ())), precision=precision, preferred_element_type=F32
    )


def split_dot(a, b):
    high = a.astype(BF16)
    low = (a - high.astype(F32)).astype(BF16)
    return dot(high, b) + dot(low, b)


def lower(n, strict=False):
    r = lax.broadcasted_iota(jnp.int32, (n, n), 0)
    c = lax.broadcasted_iota(jnp.int32, (n, n), 1)
    return r > c if strict else r >= c


def head_of_lane(heads, lanes):
    r = lax.broadcasted_iota(jnp.int32, (heads, lanes), 0)
    c = lax.broadcasted_iota(jnp.int32, (heads, lanes), 1)
    return jnp.where(c // HEADDIM == r, 1.0, 0.0).astype(BF16)


def lane_head(lanes, heads):
    r = lax.broadcasted_iota(jnp.int32, (lanes, heads), 0)
    c = lax.broadcasted_iota(jnp.int32, (lanes, heads), 1)
    return jnp.where(r // HEADDIM == c, 1.0, 0.0).astype(BF16)


def decays(ldt):
    heads, tokens = ldt.shape
    prefix = dot(lower(tokens).astype(F32), ldt, 1, 1, precision=HIGHEST)
    spread = head_of_lane(heads, heads * HEADDIM)
    grown = split_dot(jnp.exp(prefix), spread)
    left = split_dot(jnp.exp(prefix[tokens - 1 : tokens] - prefix), spread)
    return prefix, grown, left


def main_kernel(
    x_hbm, ldt_hbm, b_hbm, c_hbm, g_hbm, out_ref, dx_ref, dldt_ref, gb_ref, gc_ref,
    x_ref, ldt_ref, b_ref, c_ref, g_ref, load_sem, grown_ref, left_ref, within_ref, dxw_ref, factor, grads,
    own_in, up_in, up_out, down_in, down_out, at_owner, from_owner,
    gain_own, gain_in, gain_out, gain_at, unit_out, unit_in, full,
    up_send, up_recv, own_recv, own_send, down_recv, down_send, rep_send,
    gain_send, gain_recv, gain_far_send, gain_far_recv, unit_send, unit_recv, full_send, full_recv,
):
    heads, tokens = ldt_ref.shape
    lanes = heads * HEADDIM
    pairs = lanes // PAIR
    groups = lax.axis_size("seq") // GROUP
    peers = lax.axis_size("head")
    chunks = groups
    deep = STATE // chunks
    parts = peers // 2
    per = chunks // parts
    wide = STATE // parts
    seq, head = lax.axis_index("seq"), lax.axis_index("head")
    group, place = seq // GROUP, lax.rem(seq, GROUP)
    shift = lax.rem(head, 2) * (groups // 2)
    outer = (place == 0) | (place == GROUP - 1)
    early = jnp.where(place < GROUP // 2, 0, 1)
    late = 1 - early
    ahead = jnp.where(early == 0, 1, -1)
    e_to, l_to = (seq + ahead, head), (seq - ahead, head)

    across = 4 if groups % 16 == 0 else 1

    def owner(scan, ch):
        slot = lax.rem(ch + shift, groups)
        row, turn = lax.rem(slot, across), slot // across
        where = row * (groups // across) + lax.rem(turn + row, groups // across)
        return (jnp.where(scan == 0, where * GROUP + 1, (groups - 1 - where) * GROUP + 2), head)

    scan_owned = jnp.where(place == 1, 0, 1)
    order = jnp.where(place == 1, group, groups - 1 - group)
    row, turn = order // (groups // across), lax.rem(order, groups // across)
    turn = lax.rem(turn - row + groups, groups // across)
    mine = lax.rem(turn * across + row + groups - shift, groups)

    loads = [
        pltpu.make_async_copy(source, target, load_sem.at[i])
        for i, (source, target) in enumerate(
            ((ldt_hbm, ldt_ref), (x_hbm, x_ref), (b_hbm, b_ref), (g_hbm, g_ref), (c_hbm, c_ref))
        )
    ]
    for load in loads:
        load.start()

    barrier = pltpu.get_barrier_semaphore()

    def greet(where):
        pl.semaphore_signal(barrier, inc=1, device_id=where, device_id_type=MESH)

    @pl.when(outer)
    def _():
        def each(k, _):
            greet((k * GROUP + 1, head))
            greet((k * GROUP + 2, head))
            return 0

        lax.fori_loop(0, groups, each, 0)

    @pl.when(~outer)
    def _():
        def each(k, _):
            greet((k * GROUP, head))
            greet((k * GROUP + GROUP - 1, head))
            return 0

        lax.fori_loop(0, groups, each, 0)
        greet((jnp.where(place == 1, seq + 1, seq - 1), head))

    for step in range(1, peers):
        greet((seq, lax.rem(head + step, peers)))

    for load in loads:
        load.wait()
    ldt = ldt_ref[...]
    prefix, grown, left = decays(ldt)
    grown_ref[...] = grown
    left_ref[...] = left
    rows = dot(ldt, lower(tokens).astype(F32), 1, 1, precision=HIGHEST)
    b, c = b_ref[...], c_ref[...]
    risen = (g_ref[...].astype(F32) * grown).astype(BF16)
    scaled = (x_ref[...].astype(F32) * left).astype(BF16)
    factor[0] = risen
    factor[1] = scaled
    own_in[0] = dot(b, scaled, 0, 0).reshape(chunks, deep, lanes)
    own_in[1] = dot(c, risen, 0, 0).reshape(chunks, deep, lanes)
    for j in range(pairs):
        gain_own[j : j + 1] = grown[tokens - 1 : tokens, j * PAIR : (j + 1) * PAIR]
    gain_own[pairs:] = jnp.zeros((8 - pairs, PAIR), F32)

    scores = dot(c, b, 1, 1)
    causal = lower(tokens)
    first = lax.broadcasted_iota(jnp.int32, (tokens, PAIR), 1) < HEADDIM
    total = jnp.zeros((tokens, tokens), F32)
    for j in range(pairs):
        span = slice(j * PAIR, (j + 1) * PAIR)
        xp, gp = x_ref[:, span], g_ref[:, span]
        found = []
        for e in range(2):
            h = 2 * j + e
            decay = jnp.where(causal, jnp.exp(prefix[:, h : h + 1] - rows[h : h + 1]), 0.0)
            weighted = (scores * decay).astype(BF16)
            own = jnp.where(first if e == 0 else ~first, gp.astype(F32), 0.0).astype(BF16)
            total += dot(own, xp, 1, 1) * decay
            found.append((dot(weighted, xp), dot(weighted, gp, 0, 0)))
        within_ref[:, span] = jnp.where(first, found[0][0], found[1][0])
        dxw_ref[:, span] = jnp.where(first, found[0][1], found[1][1])
    halved = total.astype(BF16)
    grads[0] = dot(b, halved, 0, 1)
    grads[1] = dot(c, halved, 0, 0)

    @pl.when(outer)
    def _():
        pl.semaphore_wait(barrier, 2 * groups + peers - 1)

    @pl.when(~outer)
    def _():
        pl.semaphore_wait(barrier, 2 * groups + 1 + peers - 1)

    def up_copy(scan, ch, source, to):
        return pltpu.make_async_remote_copy(
            src_ref=source, dst_ref=up_in.at[scan, ch], send_sem=up_send.at[scan, ch],
            recv_sem=up_recv.at[scan, ch], device_id=to, device_id_type=MESH,
        )

    def gain_copy(scan, source, to):
        return pltpu.make_async_remote_copy(
            src_ref=source, dst_ref=gain_in.at[scan], send_sem=gain_send.at[scan],
            recv_sem=gain_recv.at[scan], device_id=to, device_id_type=MESH,
        )

    def down_copy(scan, ch, to):
        return pltpu.make_async_remote_copy(
            src_ref=down_out.at[scan, ch], dst_ref=down_in.at[scan, ch], send_sem=down_send.at[scan, ch],
            recv_sem=down_recv.at[scan, ch], device_id=to, device_id_type=MESH,
        )

    rank = jnp.where(late == 0, group, groups - 1 - group)

    def owner_copy(ch):
        return pltpu.make_async_remote_copy(
            src_ref=up_out.at[late, ch], dst_ref=at_owner.at[rank], send_sem=rep_send.at[ch],
            recv_sem=own_recv.at[rank], device_id=owner(late, ch), device_id_type=MESH,
        )

    def gain_far_copy(ch):
        return pltpu.make_async_remote_copy(
            src_ref=gain_out.at[late], dst_ref=gain_at.at[rank], send_sem=gain_far_send.at[ch],
            recv_sem=gain_far_recv.at[rank], device_id=owner(late, ch), device_id_type=MESH,
        )

    def arrived(buffer, sem, k):
        pltpu.make_async_remote_copy(
            src_ref=buffer.at[k], dst_ref=buffer.at[k], send_sem=own_send.at[k],
            recv_sem=sem.at[k], device_id=e_to, device_id_type=MESH,
        ).wait_recv()

    def back_copy(k):
        to = jnp.where(scan_owned == 0, k * GROUP, (groups - 1 - k) * GROUP + GROUP - 1)
        return pltpu.make_async_remote_copy(
            src_ref=from_owner.at[k], dst_ref=down_in.at[scan_owned, mine], send_sem=own_send.at[k],
            recv_sem=down_recv.at[scan_owned, mine], device_id=(to, head), device_id_type=MESH,
        )

    def unit_copy(u):
        return pltpu.make_async_remote_copy(
            src_ref=unit_out.at[u], dst_ref=unit_in.at[head], send_sem=unit_send.at[u],
            recv_sem=unit_recv.at[head], device_id=(seq, u), device_id_type=MESH,
        )

    def unit_from(u):
        return pltpu.make_async_remote_copy(
            src_ref=unit_in.at[u], dst_ref=unit_in.at[u], send_sem=unit_send.at[u],
            recv_sem=unit_recv.at[u], device_id=(seq, u), device_id_type=MESH,
        )

    def full_copy(u):
        return pltpu.make_async_remote_copy(
            src_ref=full.at[head], dst_ref=full.at[head], send_sem=full_send.at[u],
            recv_sem=full_recv.at[head], device_id=(seq, u), device_id_type=MESH,
        )

    def full_from(u):
        return pltpu.make_async_remote_copy(
            src_ref=full.at[u], dst_ref=full.at[u], send_sem=full_send.at[u],
            recv_sem=full_recv.at[u], device_id=(seq, u), device_id_type=MESH,
        )

    gain = jnp.concatenate([gain_own[j : j + 1] for j in range(pairs)], axis=1)

    def rise(scan, ch):
        up_copy(scan, ch, up_out.at[scan, ch], e_to).wait_recv()
        up_out[scan, ch] = own_in[scan, ch] + gain * up_in[scan, ch]

    def gain_rise(scan):
        gain_copy(scan, gain_own, e_to).wait_recv()
        gain_out[scan] = gain_own[...] * gain_in[scan]

    @pl.when(outer)
    def _():
        gain_copy(early, gain_own, e_to).start()

        def send(ch, _):
            up_copy(early, ch, own_in.at[early, ch], e_to).start()
            return 0

        lax.fori_loop(0, chunks, send, 0)
        gain_rise(late)

        def tell(ch, _):
            gain_far_copy(ch).start()
            return 0

        lax.fori_loop(0, chunks, tell, 0)

        def finish(ch, _):
            rise(late, ch)
            owner_copy(ch).start()
            return 0

        lax.fori_loop(0, chunks, finish, 0)

    lag = min(LAG, chunks)

    @pl.when(~outer)
    def _():
        gain_rise(early)
        gain_copy(early, gain_out.at[early], e_to).start()

        def step(i, _):
            @pl.when(i < chunks)
            def _():
                rise(early, i)
                up_copy(early, i, up_out.at[early, i], e_to).start()

            @pl.when(i == lag)
            def _():
                gain_rise(late)
                gain_copy(late, gain_out.at[late], l_to).start()

            @pl.when(i >= lag)
            def _():
                rise(late, i - lag)
                up_copy(late, i - lag, up_out.at[late, i - lag], l_to).start()

            return 0

        lax.fori_loop(0, chunks + lag, step, 0)

        def hand_out(k, entering):
            from_owner[k] = entering
            back_copy(k).start()
            arrived(gain_at, gain_far_recv, k)
            arrived(at_owner, own_recv, k)
            gains = jnp.concatenate([gain_at[k, j : j + 1] for j in range(pairs)], axis=1)
            return gains * entering + at_owner[k]

        lax.fori_loop(0, groups, hand_out, jnp.zeros((deep, lanes), F32))

    def landed(scan, ch):
        down_copy(scan, ch, e_to).wait_recv()

    def fall(scan, ch, to):
        landed(scan, ch)
        down_out[scan, ch] = own_in[scan, ch] + gain * down_in[scan, ch]
        down_copy(scan, ch, to).start()

    def unit(scan, ch):
        @pl.when(lax.rem(ch + 1, per) == 0)
        def _():
            q = ch // per
            u = scan * parts + q
            state = down_in[scan, pl.ds(q * per, per)].reshape(wide, lanes).astype(BF16)
            part = grads[scan, pl.ds(pl.multiple_of(q * wide, wide), wide)]
            unit_out[u] = part + dot(state, factor[scan], 1, 1)

            @pl.when(u != head)
            def _():
                unit_copy(u).start()

    @pl.when(outer)
    def _():
        def one(i, _):
            fall(early, i, e_to)
            unit(early, i)
            return 0

        lax.fori_loop(0, chunks, one, 0)

        def two(i, _):
            landed(late, i)
            unit(late, i)
            return 0

        lax.fori_loop(0, chunks, two, 0)

    @pl.when(~outer)
    def _():
        def step(i, _):
            @pl.when(i < chunks)
            def _():
                fall(early, i, e_to)

            @pl.when(i >= lag)
            def _():
                fall(late, i - lag, l_to)

            @pl.when(i < chunks)
            def _():
                unit(early, i)

            @pl.when(i >= lag)
            def _():
                unit(late, i - lag)

            return 0

        lax.fori_loop(0, chunks + lag, step, 0)

    spread = lane_head(lanes, heads)
    rising = jnp.zeros((tokens, heads), F32)
    falling = jnp.zeros((tokens, heads), F32)
    start = down_in[0].reshape(STATE, lanes)
    adj = down_in[1].reshape(STATE, lanes)
    for j in range(pairs):
        span = slice(j * PAIR, (j + 1) * PAIR)
        x, g = x_ref[:, span].astype(F32), g_ref[:, span].astype(F32)
        own = spread[span]
        out = within_ref[:, span] + grown_ref[:, span] * dot(c, start[:, span].astype(BF16))
        pushed = left_ref[:, span] * dot(b, adj[:, span].astype(BF16))
        out_ref[:, span] = out.astype(BF16)
        dx_ref[:, span] = (dxw_ref[:, span] + pushed).astype(BF16)
        rising += split_dot(g * out - x * dxw_ref[:, span], own)
        falling += split_dot(x * pushed, own)

    def add(o, total):
        u = lax.rem(head + o, peers)
        unit_from(u).wait_recv()
        return total + unit_in[u]

    full[head] = lax.fori_loop(1, peers, add, unit_out[head])
    for o in range(1, peers):
        full_copy(lax.rem(head + o, peers)).start()

    meet = jnp.sum(start * adj, axis=0, keepdims=True) * gain
    meet = jnp.broadcast_to(meet, (8, lanes))
    high = meet.astype(BF16)
    low = (meet - high.astype(F32)).astype(BF16)
    where = head_of_lane(heads, lanes)
    last = dot(where, high, 1, 1) + dot(where, low, 1, 1)
    dldt_ref[...] = (
        dot(rising, lower(tokens).astype(F32), 0, 0, precision=HIGHEST)
        + dot(falling, lower(tokens, True).astype(F32), 0, 1, precision=HIGHEST)
        + last[:, :1]
    )

    gain_copy(early, gain_own, e_to).wait_send()

    def gone(ch, _):
        up_copy(early, ch, up_out.at[early, ch], e_to).wait_send()
        down_copy(early, ch, e_to).wait_send()

        @pl.when(outer)
        def _():
            owner_copy(ch).wait_send()
            gain_far_copy(ch).wait_send()

        @pl.when(~outer)
        def _():
            up_copy(late, ch, up_out.at[late, ch], l_to).wait_send()
            down_copy(late, ch, l_to).wait_send()
            back_copy(ch).wait_send()

        return 0

    lax.fori_loop(0, chunks, gone, 0)

    @pl.when(~outer)
    def _():
        gain_copy(late, gain_own, l_to).wait_send()

    for o in range(1, peers):
        u = lax.rem(head + o, peers)
        unit_copy(u).wait_send()
        full_copy(u).wait_send()
        full_from(u).wait_recv()
    gc_ref[...] = full[:parts].reshape(STATE, tokens).T
    gb_ref[...] = full[parts:].reshape(STATE, tokens).T


def store_kernel(*refs):
    sems = refs[-1]
    copies = [pltpu.make_async_copy(refs[i], refs[5 + i], sems.at[i]) for i in range(5)]
    for copy in copies:
        copy.start()
    for copy in copies:
        copy.wait()


def shards(inputs, log_decay, b_proj, c_proj, grad_out):
    tokens, heads = log_decay.shape
    lanes = heads * HEADDIM
    groups = lax.axis_size("seq") // GROUP
    peers = lax.axis_size("head")
    deep = STATE // groups
    unit = (peers, STATE // (peers // 2), tokens)
    chunk = (2, groups, deep, lanes)
    dma = pltpu.SemaphoreType.DMA
    half = jax.ShapeDtypeStruct(inputs.shape, BF16)
    thin = jax.ShapeDtypeStruct((tokens, STATE), F32)
    whole = pl.BlockSpec(memory_space=VMEM)
    results = (half, half, jax.ShapeDtypeStruct((heads, tokens), F32), thin, thin)
    held = pl.pallas_call(
        main_kernel,
        out_shape=tuple(pltpu.VMEM(a.shape, a.dtype) for a in results),
        in_specs=[pl.BlockSpec(memory_space=pl.ANY)] * 5,
        out_specs=(whole,) * 5,
        scratch_shapes=[
            pltpu.VMEM((tokens, lanes), BF16), pltpu.VMEM((heads, tokens), F32),
            pltpu.VMEM((tokens, STATE), BF16), pltpu.VMEM((tokens, STATE), BF16),
            pltpu.VMEM((tokens, lanes), BF16), dma((5,)),
            pltpu.VMEM((tokens, lanes), F32), pltpu.VMEM((tokens, lanes), F32),
            pltpu.VMEM((tokens, lanes), F32), pltpu.VMEM((tokens, lanes), F32),
            pltpu.VMEM((2, tokens, lanes), BF16), pltpu.VMEM((2, STATE, tokens), F32),
            pltpu.VMEM(chunk, F32), pltpu.VMEM(chunk, F32), pltpu.VMEM(chunk, F32),
            pltpu.VMEM(chunk, F32), pltpu.VMEM(chunk, F32),
            pltpu.VMEM((groups, deep, lanes), F32), pltpu.VMEM((groups, deep, lanes), F32),
            pltpu.VMEM((8, PAIR), F32), pltpu.VMEM((2, 8, PAIR), F32), pltpu.VMEM((2, 8, PAIR), F32),
            pltpu.VMEM((groups, 8, PAIR), F32),
            pltpu.VMEM(unit, F32), pltpu.VMEM(unit, F32), pltpu.VMEM(unit, F32),
            dma((2, groups)), dma((2, groups)), dma((groups,)), dma((groups,)),
            dma((2, groups)), dma((2, groups)), dma((groups,)),
            dma((2,)), dma((2,)), dma((groups,)), dma((groups,)),
            dma((peers,)), dma((peers,)), dma((peers,)), dma((peers,)),
        ],
        compiler_params=pltpu.CompilerParams(
            collective_id=0, has_side_effects=True, vmem_limit_bytes=56 * 2**20
        ),
        name="scan",
    )(inputs, log_decay.T, b_proj, c_proj, grad_out)
    outputs, grad_inputs, grad_decay, grad_b, grad_c = pl.pallas_call(
        store_kernel,
        out_shape=results,
        in_specs=[pl.BlockSpec(memory_space=pl.ANY)] * 5,
        out_specs=(pl.BlockSpec(memory_space=pl.ANY),) * 5,
        scratch_shapes=[dma((5,))],
        name="store",
    )(*(pltpu.with_memory_space_constraint(array, VMEM) for array in held))
    return outputs, grad_inputs, grad_decay.T, grad_b, grad_c


def solution(mesh):
    placed = (P("seq", "head"), P("seq", "head"), P("seq", None), P("seq", None), P("seq", "head"))
    return jax.shard_map(
        shards,
        mesh=mesh,
        in_specs=placed,
        out_specs=(
            P("seq", "head"),
            P("seq", "head"),
            P("seq", "head"),
            P("seq", None),
            P("seq", None),
        ),
        check_vma=False,
    )
```

```python
import jax
import jax.numpy as jnp
from jax import lax
from jax.experimental import pallas as pl
from jax.experimental.pallas import tpu as pltpu
from jax.sharding import PartitionSpec as P

HEADDIM = 64
STATE = 128
PAIR = 128
GROUP = 4
LAG = 6
MESH = pl.DeviceIdType.MESH
F32 = jnp.float32
BF16 = jnp.bfloat16
VMEM = pltpu.MemorySpace.VMEM
HIGHEST = lax.Precision.HIGHEST


def dot(a, b, da=1, db=0, precision=None):
    return lax.dot_general(
        a, b, (((da,), (db,)), ((), ())), precision=precision, preferred_element_type=F32
    )


def split_dot(a, b):
    high = a.astype(BF16)
    low = (a - high.astype(F32)).astype(BF16)
    return dot(high, b) + dot(low, b)


def lower(n, strict=False):
    r = lax.broadcasted_iota(jnp.int32, (n, n), 0)
    c = lax.broadcasted_iota(jnp.int32, (n, n), 1)
    return r > c if strict else r >= c


def head_of_lane(heads, lanes):
    r = lax.broadcasted_iota(jnp.int32, (heads, lanes), 0)
    c = lax.broadcasted_iota(jnp.int32, (heads, lanes), 1)
    return jnp.where(c // HEADDIM == r, 1.0, 0.0).astype(BF16)


def lane_head(lanes, heads):
    r = lax.broadcasted_iota(jnp.int32, (lanes, heads), 0)
    c = lax.broadcasted_iota(jnp.int32, (lanes, heads), 1)
    return jnp.where(r // HEADDIM == c, 1.0, 0.0).astype(BF16)


def decays(ldt):
    heads, tokens = ldt.shape
    prefix = dot(lower(tokens).astype(F32), ldt, 1, 1, precision=HIGHEST)
    spread = head_of_lane(heads, heads * HEADDIM)
    grown = split_dot(jnp.exp(prefix), spread)
    left = split_dot(jnp.exp(prefix[tokens - 1 : tokens] - prefix), spread)
    return prefix, grown, left


def main_kernel(
    x_hbm, ldt_hbm, b_hbm, c_hbm, g_hbm, out_ref, dx_ref, dldt_ref, gb_ref, gc_ref,
    x_ref, ldt_ref, b_ref, c_ref, g_ref, load_sem, grown_ref, left_ref, within_ref, dxw_ref, factor, grads,
    own_in, up_in, up_out, down_in, down_out, at_owner, from_owner,
    gain_own, gain_in, gain_out, gain_at, gain_wide, unit_out, unit_in, full, last_in,
    up_send, up_recv, own_recv, own_send, down_recv, down_send, rep_send,
    gain_send, gain_recv, gain_far_send, gain_far_recv, unit_send, unit_recv, full_send, full_recv, last_send, last_recv,
):
    heads, tokens = ldt_ref.shape
    lanes = heads * HEADDIM
    pairs = lanes // PAIR
    groups = lax.axis_size("seq") // GROUP
    peers = lax.axis_size("head")
    chunks = groups
    deep = STATE // chunks
    parts = peers // 2
    per = chunks // parts
    wide = STATE // parts
    seq, head = lax.axis_index("seq"), lax.axis_index("head")
    group, place = seq // GROUP, lax.rem(seq, GROUP)
    shift = lax.rem(head, 2) * (groups // 2)
    outer = (place == 0) | (place == GROUP - 1)
    early = jnp.where(place < GROUP // 2, 0, 1)
    late = 1 - early
    ahead = jnp.where(early == 0, 1, -1)
    e_to, l_to = (seq + ahead, head), (seq - ahead, head)

    across = 4 if groups % 16 == 0 else 1

    def owner(scan, ch):
        slot = lax.rem(ch + shift, groups)
        row, turn = lax.rem(slot, across), slot // across
        where = row * (groups // across) + lax.rem(turn + row, groups // across)
        return (jnp.where(scan == 0, where * GROUP + 1, (groups - 1 - where) * GROUP + 2), head)

    scan_owned = jnp.where(place == 1, 0, 1)
    order = jnp.where(place == 1, group, groups - 1 - group)
    row, turn = order // (groups // across), lax.rem(order, groups // across)
    turn = lax.rem(turn - row + groups, groups // across)
    mine = lax.rem(turn * across + row + groups - shift, groups)

    loads = [
        pltpu.make_async_copy(source, target, load_sem.at[i])
        for i, (source, target) in enumerate(
            ((ldt_hbm, ldt_ref), (x_hbm, x_ref), (b_hbm, b_ref), (g_hbm, g_ref), (c_hbm, c_ref))
        )
    ]
    for load in loads:
        load.start()

    barrier = pltpu.get_barrier_semaphore()

    def greet(where):
        pl.semaphore_signal(barrier, inc=1, device_id=where, device_id_type=MESH)

    @pl.when(outer)
    def _():
        def each(k, _):
            greet((k * GROUP + 1, head))
            greet((k * GROUP + 2, head))
            return 0

        lax.fori_loop(0, groups, each, 0)

    @pl.when(~outer)
    def _():
        def each(k, _):
            greet((k * GROUP, head))
            greet((k * GROUP + GROUP - 1, head))
            return 0

        lax.fori_loop(0, groups, each, 0)
        greet((jnp.where(place == 1, seq + 1, seq - 1), head))

    for step in range(1, peers):
        greet((seq, lax.rem(head + step, peers)))

    for load in loads:
        load.wait()
    ldt = ldt_ref[...]
    prefix, grown, left = decays(ldt)
    grown_ref[...] = grown
    left_ref[...] = left
    rows = dot(ldt, lower(tokens).astype(F32), 1, 1, precision=HIGHEST)
    b, c = b_ref[...], c_ref[...]
    risen = (g_ref[...].astype(F32) * grown).astype(BF16)
    scaled = (x_ref[...].astype(F32) * left).astype(BF16)
    factor[0] = risen
    factor[1] = scaled
    own_in[0] = dot(b, scaled, 0, 0).reshape(chunks, deep, lanes)
    own_in[1] = dot(c, risen, 0, 0).reshape(chunks, deep, lanes)
    gain = grown[tokens - 1 : tokens]
    gain_own[...] = jnp.concatenate(
        [jnp.exp(prefix[tokens - 1 : tokens]), jnp.zeros((1, PAIR - heads), F32)], axis=1
    )

    def attend():
        scores = dot(c, b, 1, 1)
        causal = lower(tokens)
        first = lax.broadcasted_iota(jnp.int32, (tokens, PAIR), 1) < HEADDIM
        total = jnp.zeros((tokens, tokens), F32)
        for j in range(pairs):
            span = slice(j * PAIR, (j + 1) * PAIR)
            xp, gp = x_ref[:, span], g_ref[:, span]
            found = []
            for e in range(2):
                h = 2 * j + e
                decay = jnp.where(causal, jnp.exp(prefix[:, h : h + 1] - rows[h : h + 1]), 0.0)
                weighted = (scores * decay).astype(BF16)
                own = jnp.where(first if e == 0 else ~first, gp.astype(F32), 0.0).astype(BF16)
                total += dot(own, xp, 1, 1) * decay
                found.append((dot(weighted, xp), dot(weighted, gp, 0, 0)))
            within_ref[:, span] = jnp.where(first, found[0][0], found[1][0])
            dxw_ref[:, span] = jnp.where(first, found[0][1], found[1][1])
        halved = total.astype(BF16)
        grads[0] = dot(b, halved, 0, 1)
        grads[1] = dot(c, halved, 0, 0)

    second = lax.rem(head, 2) == 1

    @pl.when(~second)
    def _():
        attend()

    @pl.when(outer)
    def _():
        pl.semaphore_wait(barrier, 2 * groups + peers - 1)

    @pl.when(~outer)
    def _():
        pl.semaphore_wait(barrier, 2 * groups + 1 + peers - 1)

    @pl.when(second)
    def _():
        attend()

    def up_copy(scan, ch, source, to):
        return pltpu.make_async_remote_copy(
            src_ref=source, dst_ref=up_in.at[scan, ch], send_sem=up_send.at[scan, ch],
            recv_sem=up_recv.at[scan, ch], device_id=to, device_id_type=MESH,
        )

    def gain_copy(scan, source, to):
        return pltpu.make_async_remote_copy(
            src_ref=source, dst_ref=gain_in.at[scan], send_sem=gain_send.at[scan],
            recv_sem=gain_recv.at[scan], device_id=to, device_id_type=MESH,
        )

    def down_copy(scan, ch, to):
        return pltpu.make_async_remote_copy(
            src_ref=down_out.at[scan, ch], dst_ref=down_in.at[scan, ch], send_sem=down_send.at[scan, ch],
            recv_sem=down_recv.at[scan, ch], device_id=to, device_id_type=MESH,
        )

    rank = jnp.where(late == 0, group, groups - 1 - group)

    def owner_copy(ch):
        return pltpu.make_async_remote_copy(
            src_ref=up_out.at[late, ch], dst_ref=at_owner.at[rank], send_sem=rep_send.at[ch],
            recv_sem=own_recv.at[rank], device_id=owner(late, ch), device_id_type=MESH,
        )

    def gain_far_copy(ch):
        return pltpu.make_async_remote_copy(
            src_ref=gain_out.at[late], dst_ref=gain_at.at[rank], send_sem=gain_far_send.at[ch],
            recv_sem=gain_far_recv.at[rank], device_id=owner(late, ch), device_id_type=MESH,
        )

    def arrived(buffer, sem, k):
        pltpu.make_async_remote_copy(
            src_ref=buffer.at[k], dst_ref=buffer.at[k], send_sem=own_send.at[k],
            recv_sem=sem.at[k], device_id=e_to, device_id_type=MESH,
        ).wait_recv()

    def back_copy(k):
        to = jnp.where(scan_owned == 0, k * GROUP, (groups - 1 - k) * GROUP + GROUP - 1)
        return pltpu.make_async_remote_copy(
            src_ref=from_owner.at[k], dst_ref=down_in.at[scan_owned, mine], send_sem=own_send.at[k],
            recv_sem=down_recv.at[scan_owned, mine], device_id=(to, head), device_id_type=MESH,
        )

    def unit_copy(u):
        return pltpu.make_async_remote_copy(
            src_ref=unit_out.at[u], dst_ref=unit_in.at[head], send_sem=unit_send.at[u],
            recv_sem=unit_recv.at[head], device_id=(seq, u), device_id_type=MESH,
        )

    def unit_from(u):
        return pltpu.make_async_remote_copy(
            src_ref=unit_in.at[u], dst_ref=unit_in.at[u], send_sem=unit_send.at[u],
            recv_sem=unit_recv.at[u], device_id=(seq, u), device_id_type=MESH,
        )

    final = late * parts + parts - 1

    def last_copy(u):
        return pltpu.make_async_remote_copy(
            src_ref=unit_out.at[final], dst_ref=last_in.at[head], send_sem=last_send.at[u],
            recv_sem=last_recv.at[head], device_id=(seq, u), device_id_type=MESH,
        )

    def last_from(u):
        return pltpu.make_async_remote_copy(
            src_ref=last_in.at[u], dst_ref=last_in.at[u], send_sem=last_send.at[u],
            recv_sem=last_recv.at[u], device_id=(seq, u), device_id_type=MESH,
        )

    def full_copy(u):
        return pltpu.make_async_remote_copy(
            src_ref=full.at[head], dst_ref=full.at[head], send_sem=full_send.at[u],
            recv_sem=full_recv.at[head], device_id=(seq, u), device_id_type=MESH,
        )

    def full_from(u):
        return pltpu.make_async_remote_copy(
            src_ref=full.at[u], dst_ref=full.at[u], send_sem=full_send.at[u],
            recv_sem=full_recv.at[u], device_id=(seq, u), device_id_type=MESH,
        )

    def rise(scan, ch):
        up_copy(scan, ch, up_out.at[scan, ch], e_to).wait_recv()
        up_out[scan, ch] = own_in[scan, ch] + gain * up_in[scan, ch]

    def gain_rise(scan):
        gain_copy(scan, gain_own, e_to).wait_recv()
        gain_out[scan] = gain_own[...] * gain_in[scan]

    @pl.when(outer)
    def _():
        gain_copy(early, gain_own, e_to).start()

        def send(ch, _):
            up_copy(early, ch, own_in.at[early, ch], e_to).start()
            return 0

        lax.fori_loop(0, chunks, send, 0)
        gain_rise(late)

        def tell(ch, _):
            @pl.when(rank < groups - 1)
            def _():
                gain_far_copy(ch).start()

            return 0

        lax.fori_loop(0, chunks, tell, 0)

        def finish(ch, _):
            rise(late, ch)

            @pl.when(rank < groups - 1)
            def _():
                owner_copy(ch).start()

            return 0

        lax.fori_loop(0, chunks, finish, 0)

    lag = min(LAG, chunks)

    @pl.when(~outer)
    def _():
        gain_rise(early)
        gain_copy(early, gain_out.at[early], e_to).start()

        def step(i, _):
            @pl.when(i < chunks)
            def _():
                rise(early, i)
                up_copy(early, i, up_out.at[early, i], e_to).start()

            @pl.when(i == lag)
            def _():
                gain_rise(late)
                gain_copy(late, gain_out.at[late], l_to).start()

            @pl.when(i >= lag)
            def _():
                rise(late, i - lag)
                up_copy(late, i - lag, up_out.at[late, i - lag], l_to).start()

            return 0

        lax.fori_loop(0, chunks + lag, step, 0)

        def told(k, _):
            arrived(gain_at, gain_far_recv, k)
            return 0

        lax.fori_loop(0, groups - 1, told, 0)
        gain_at[groups - 1] = jnp.zeros((1, PAIR), F32)
        gains = jnp.concatenate([gain_at[k] for k in range(groups)], axis=0)
        r = lax.broadcasted_iota(jnp.int32, (PAIR, lanes), 0)
        l = lax.broadcasted_iota(jnp.int32, (PAIR, lanes), 1)
        gain_wide[...] = split_dot(gains, jnp.where(l // HEADDIM == r, 1.0, 0.0).astype(BF16))
        arrived(at_owner, own_recv, 0)

        def hand_out(k, entering):
            from_owner[k] = entering
            back_copy(k).start()

            @pl.when(k < groups - 1)
            def _():
                arrived(at_owner, own_recv, k)

            return gain_wide[pl.ds(k, 1)] * entering + at_owner[k]

        at_owner[groups - 1] = jnp.zeros((deep, lanes), F32)
        lax.fori_loop(1, groups, hand_out, at_owner[0])

    def landed(scan, ch):
        down_copy(scan, ch, e_to).wait_recv()

    begins = jnp.where(early == 0, group, groups - 1 - group) == 0

    def fall(scan, ch, to):
        down_out[scan, ch] = own_in[scan, ch] + gain * down_in[scan, ch]
        down_copy(scan, ch, to).start()

    def unit(scan, ch):
        @pl.when(lax.rem(ch + 1, per) == 0)
        def _():
            q = ch // per
            u = scan * parts + q
            state = down_in[scan, pl.ds(q * per, per)].reshape(wide, lanes).astype(BF16)
            part = grads[scan, pl.ds(pl.multiple_of(q * wide, wide), wide)]
            unit_out[u] = part + dot(state, factor[scan], 1, 1)

            @pl.when((u != head) & (u != final))
            def _():
                unit_copy(u).start()

            @pl.when(u == final)
            def _():
                for o in range(1, peers):
                    last_copy(lax.rem(head + o, peers)).start()

    @pl.when(outer)
    def _():
        def one(i, _):
            @pl.when(begins)
            def _():
                down_in[early, i] = jnp.zeros((deep, lanes), F32)

            @pl.when(~begins)
            def _():
                landed(early, i)

            fall(early, i, e_to)
            unit(early, i)
            return 0

        lax.fori_loop(0, chunks, one, 0)

        def two(i, _):
            landed(late, i)
            unit(late, i)
            return 0

        lax.fori_loop(0, chunks, two, 0)

    @pl.when(~outer)
    def _():
        def step(i, _):
            @pl.when(i < chunks)
            def _():
                landed(early, i)
                fall(early, i, e_to)

            @pl.when(i >= lag)
            def _():
                landed(late, i - lag)
                fall(late, i - lag, l_to)

            @pl.when(i < chunks)
            def _():
                unit(early, i)

            @pl.when(i >= lag)
            def _():
                unit(late, i - lag)

            return 0

        lax.fori_loop(0, chunks + lag, step, 0)

    spread = lane_head(lanes, heads)
    rising = jnp.zeros((tokens, heads), F32)
    falling = jnp.zeros((tokens, heads), F32)
    start = down_in[0].reshape(STATE, lanes)
    adj = down_in[1].reshape(STATE, lanes)
    @pl.when(head != final)
    def _():
        def add(o, total):
            u = lax.rem(head + o, peers)
            unit_from(u).wait_recv()
            return total + unit_in[u]

        full[head] = lax.fori_loop(1, peers, add, unit_out[head])
        for o in range(1, peers):
            full_copy(lax.rem(head + o, peers)).start()

    for j in range(pairs):
        span = slice(j * PAIR, (j + 1) * PAIR)
        x, g = x_ref[:, span].astype(F32), g_ref[:, span].astype(F32)
        own = spread[span]
        out = within_ref[:, span] + grown_ref[:, span] * dot(c, start[:, span].astype(BF16))
        pushed = left_ref[:, span] * dot(b, adj[:, span].astype(BF16))
        out_ref[:, span] = out.astype(BF16)
        dx_ref[:, span] = (dxw_ref[:, span] + pushed).astype(BF16)
        rising += split_dot(g * out - x * dxw_ref[:, span], own)
        falling += split_dot(x * pushed, own)

    meet = jnp.sum(start * adj, axis=0, keepdims=True) * gain
    meet = jnp.broadcast_to(meet, (8, lanes))
    high = meet.astype(BF16)
    low = (meet - high.astype(F32)).astype(BF16)
    where = head_of_lane(heads, lanes)
    last = dot(where, high, 1, 1) + dot(where, low, 1, 1)
    dldt_ref[...] = (
        dot(rising, lower(tokens).astype(F32), 0, 0, precision=HIGHEST)
        + dot(falling, lower(tokens, True).astype(F32), 0, 1, precision=HIGHEST)
        + last[:, :1]
    )

    gain_copy(early, gain_own, e_to).wait_send()

    def gone(ch, _):
        up_copy(early, ch, up_out.at[early, ch], e_to).wait_send()
        down_copy(early, ch, e_to).wait_send()

        @pl.when(outer)
        def _():
            @pl.when(rank < groups - 1)
            def _():
                owner_copy(ch).wait_send()
                gain_far_copy(ch).wait_send()

        @pl.when(~outer)
        def _():
            up_copy(late, ch, up_out.at[late, ch], l_to).wait_send()
            down_copy(late, ch, l_to).wait_send()

            @pl.when(ch > 0)
            def _():
                back_copy(ch).wait_send()

        return 0

    lax.fori_loop(0, chunks, gone, 0)

    @pl.when(~outer)
    def _():
        gain_copy(late, gain_own, l_to).wait_send()

    last_in[head] = unit_out[final]
    for o in range(1, peers):
        u = lax.rem(head + o, peers)
        last_copy(u).wait_send()
        last_from(u).wait_recv()

        @pl.when(u != final)
        def _():
            unit_copy(u).wait_send()
            full_from(u).wait_recv()

        @pl.when(head != final)
        def _():
            full_copy(u).wait_send()

    total = last_in[0]
    for u in range(1, peers):
        total += last_in[u]
    full[final] = total
    gc_ref[...] = full[:parts].reshape(STATE, tokens).T
    gb_ref[...] = full[parts:].reshape(STATE, tokens).T


def store_kernel(*refs):
    sems = refs[-1]
    copies = [pltpu.make_async_copy(refs[i], refs[5 + i], sems.at[i]) for i in range(5)]
    for copy in copies:
        copy.start()
    for copy in copies:
        copy.wait()


def shards(inputs, log_decay, b_proj, c_proj, grad_out):
    tokens, heads = log_decay.shape
    lanes = heads * HEADDIM
    groups = lax.axis_size("seq") // GROUP
    peers = lax.axis_size("head")
    deep = STATE // groups
    unit = (peers, STATE // (peers // 2), tokens)
    chunk = (2, groups, deep, lanes)
    dma = pltpu.SemaphoreType.DMA
    half = jax.ShapeDtypeStruct(inputs.shape, BF16)
    thin = jax.ShapeDtypeStruct((tokens, STATE), F32)
    whole = pl.BlockSpec(memory_space=VMEM)
    results = (half, half, jax.ShapeDtypeStruct((heads, tokens), F32), thin, thin)
    held = pl.pallas_call(
        main_kernel,
        out_shape=tuple(pltpu.VMEM(a.shape, a.dtype) for a in results),
        in_specs=[pl.BlockSpec(memory_space=pl.ANY)] * 5,
        out_specs=(whole,) * 5,
        scratch_shapes=[
            pltpu.VMEM((tokens, lanes), BF16), pltpu.VMEM((heads, tokens), F32),
            pltpu.VMEM((tokens, STATE), BF16), pltpu.VMEM((tokens, STATE), BF16),
            pltpu.VMEM((tokens, lanes), BF16), dma((5,)),
            pltpu.VMEM((tokens, lanes), F32), pltpu.VMEM((tokens, lanes), F32),
            pltpu.VMEM((tokens, lanes), F32), pltpu.VMEM((tokens, lanes), F32),
            pltpu.VMEM((2, tokens, lanes), BF16), pltpu.VMEM((2, STATE, tokens), F32),
            pltpu.VMEM(chunk, F32), pltpu.VMEM(chunk, F32), pltpu.VMEM(chunk, F32),
            pltpu.VMEM(chunk, F32), pltpu.VMEM(chunk, F32),
            pltpu.VMEM((groups, deep, lanes), F32), pltpu.VMEM((groups, deep, lanes), F32),
            pltpu.VMEM((1, PAIR), F32), pltpu.VMEM((2, 1, PAIR), F32), pltpu.VMEM((2, 1, PAIR), F32),
            pltpu.VMEM((groups, 1, PAIR), F32), pltpu.VMEM((groups, lanes), F32),
            pltpu.VMEM(unit, F32), pltpu.VMEM(unit, F32), pltpu.VMEM(unit, F32), pltpu.VMEM(unit, F32),
            dma((2, groups)), dma((2, groups)), dma((groups,)), dma((groups,)),
            dma((2, groups)), dma((2, groups)), dma((groups,)),
            dma((2,)), dma((2,)), dma((groups,)), dma((groups,)),
            dma((peers,)), dma((peers,)), dma((peers,)), dma((peers,)), dma((peers,)), dma((peers,)),
        ],
        compiler_params=pltpu.CompilerParams(
            collective_id=0, has_side_effects=True, vmem_limit_bytes=56 * 2**20
        ),
        name="scan",
    )(inputs, log_decay.T, b_proj, c_proj, grad_out)
    outputs, grad_inputs, grad_decay, grad_b, grad_c = pl.pallas_call(
        store_kernel,
        out_shape=results,
        in_specs=[pl.BlockSpec(memory_space=pl.ANY)] * 5,
        out_specs=(pl.BlockSpec(memory_space=pl.ANY),) * 5,
        scratch_shapes=[dma((5,))],
        name="store",
    )(*(pltpu.with_memory_space_constraint(array, VMEM) for array in held))
    return outputs, grad_inputs, grad_decay.T, grad_b, grad_c


def solution(mesh):
    placed = (P("seq", "head"), P("seq", "head"), P("seq", None), P("seq", None), P("seq", "head"))
    return jax.shard_map(
        shards,
        mesh=mesh,
        in_specs=placed,
        out_specs=(
            P("seq", "head"),
            P("seq", "head"),
            P("seq", "head"),
            P("seq", None),
            P("seq", None),
        ),
        check_vma=False,
    )
```

```python
import jax
import jax.numpy as jnp
from jax import lax
from jax.experimental import pallas as pl
from jax.experimental.pallas import tpu as pltpu
from jax.sharding import PartitionSpec as P

HEADDIM = 64
STATE = 128
PAIR = 128
GROUP = 4
LAG = 6
MESH = pl.DeviceIdType.MESH
F32 = jnp.float32
BF16 = jnp.bfloat16
VMEM = pltpu.MemorySpace.VMEM
HIGHEST = lax.Precision.HIGHEST


def dot(a, b, da=1, db=0, precision=None):
    return lax.dot_general(
        a, b, (((da,), (db,)), ((), ())), precision=precision, preferred_element_type=F32
    )


def split_dot(a, b):
    high = a.astype(BF16)
    low = (a - high.astype(F32)).astype(BF16)
    return dot(high, b) + dot(low, b)


def lower(n, strict=False):
    r = lax.broadcasted_iota(jnp.int32, (n, n), 0)
    c = lax.broadcasted_iota(jnp.int32, (n, n), 1)
    return r > c if strict else r >= c


def head_of_lane(heads, lanes):
    r = lax.broadcasted_iota(jnp.int32, (heads, lanes), 0)
    c = lax.broadcasted_iota(jnp.int32, (heads, lanes), 1)
    return jnp.where(c // HEADDIM == r, 1.0, 0.0).astype(BF16)


def lane_head(lanes, heads):
    r = lax.broadcasted_iota(jnp.int32, (lanes, heads), 0)
    c = lax.broadcasted_iota(jnp.int32, (lanes, heads), 1)
    return jnp.where(r // HEADDIM == c, 1.0, 0.0).astype(BF16)


def decays(ldt):
    heads, tokens = ldt.shape
    prefix = dot(lower(tokens).astype(F32), ldt, 1, 1, precision=HIGHEST)
    spread = head_of_lane(heads, heads * HEADDIM)
    grown = split_dot(jnp.exp(prefix), spread)
    left = split_dot(jnp.exp(prefix[tokens - 1 : tokens] - prefix), spread)
    return prefix, grown, left


def main_kernel(
    x_hbm, ldt_hbm, b_hbm, c_hbm, g_hbm, out_ref, dx_ref, dldt_ref, gb_ref, gc_ref,
    x_ref, ldt_ref, b_ref, c_ref, g_ref, load_sem, grown_ref, left_ref, within_ref, dxw_ref, factor, grads,
    own_in, up_in, up_out, down_in, down_out, at_owner, from_owner,
    gain_own, gain_in, gain_out, gain_at, gain_wide, unit_out, unit_in, full, last_in,
    up_send, up_recv, own_recv, own_send, down_recv, down_send, rep_send,
    gain_send, gain_recv, gain_far_send, gain_far_recv, unit_send, unit_recv, full_send, full_recv, last_send, last_recv,
):
    heads, tokens = ldt_ref.shape
    lanes = heads * HEADDIM
    pairs = lanes // PAIR
    groups = lax.axis_size("seq") // GROUP
    peers = lax.axis_size("head")
    chunks = groups
    deep = STATE // chunks
    parts = peers // 2
    per = chunks // parts
    wide = STATE // parts
    seq, head = lax.axis_index("seq"), lax.axis_index("head")
    group, place = seq // GROUP, lax.rem(seq, GROUP)
    shift = lax.rem(head, 2) * (groups // 2)
    outer = (place == 0) | (place == GROUP - 1)
    early = jnp.where(place < GROUP // 2, 0, 1)
    late = 1 - early
    ahead = jnp.where(early == 0, 1, -1)
    e_to, l_to = (seq + ahead, head), (seq - ahead, head)

    across = 4 if groups % 16 == 0 else 1

    def owner(scan, ch):
        slot = lax.rem(ch + shift, groups)
        row, turn = lax.rem(slot, across), slot // across
        where = row * (groups // across) + lax.rem(turn + row, groups // across)
        return (jnp.where(scan == 0, where * GROUP + 1, (groups - 1 - where) * GROUP + 2), head)

    scan_owned = jnp.where(place == 1, 0, 1)
    order = jnp.where(place == 1, group, groups - 1 - group)
    row, turn = order // (groups // across), lax.rem(order, groups // across)
    turn = lax.rem(turn - row + groups, groups // across)
    mine = lax.rem(turn * across + row + groups - shift, groups)

    loads = [
        pltpu.make_async_copy(source, target, load_sem.at[i])
        for i, (source, target) in enumerate(
            ((ldt_hbm, ldt_ref), (x_hbm, x_ref), (b_hbm, b_ref), (g_hbm, g_ref), (c_hbm, c_ref))
        )
    ]
    for load in loads:
        load.start()

    barrier = pltpu.get_barrier_semaphore()

    def greet(where):
        pl.semaphore_signal(barrier, inc=1, device_id=where, device_id_type=MESH)

    @pl.when(outer)
    def _():
        def each(k, _):
            greet((k * GROUP + 1, head))
            greet((k * GROUP + 2, head))
            return 0

        lax.fori_loop(0, groups, each, 0)

    @pl.when(~outer)
    def _():
        def each(k, _):
            greet((k * GROUP, head))
            greet((k * GROUP + GROUP - 1, head))
            return 0

        lax.fori_loop(0, groups, each, 0)
        greet((jnp.where(place == 1, seq + 1, seq - 1), head))

    for step in range(1, peers):
        greet((seq, lax.rem(head + step, peers)))

    for load in loads:
        load.wait()
    ldt = ldt_ref[...]
    prefix, grown, left = decays(ldt)
    grown_ref[...] = grown
    left_ref[...] = left
    rows = dot(ldt, lower(tokens).astype(F32), 1, 1, precision=HIGHEST)
    b, c = b_ref[...], c_ref[...]
    risen = (g_ref[...].astype(F32) * grown).astype(BF16)
    scaled = (x_ref[...].astype(F32) * left).astype(BF16)
    factor[0] = risen
    factor[1] = scaled
    own_in[0] = dot(b, scaled, 0, 0).reshape(chunks, deep, lanes)
    own_in[1] = dot(c, risen, 0, 0).reshape(chunks, deep, lanes)
    gain = grown[tokens - 1 : tokens]
    gain_own[...] = jnp.concatenate(
        [jnp.exp(prefix[tokens - 1 : tokens]), jnp.zeros((1, PAIR - heads), F32)], axis=1
    )

    def attend():
        scores = dot(c, b, 1, 1)
        causal = lower(tokens)
        first = lax.broadcasted_iota(jnp.int32, (tokens, PAIR), 1) < HEADDIM
        total = jnp.zeros((tokens, tokens), F32)
        for j in range(pairs):
            span = slice(j * PAIR, (j + 1) * PAIR)
            xp, gp = x_ref[:, span], g_ref[:, span]
            found = []
            for e in range(2):
                h = 2 * j + e
                decay = jnp.where(causal, jnp.exp(prefix[:, h : h + 1] - rows[h : h + 1]), 0.0)
                weighted = (scores * decay).astype(BF16)
                own = jnp.where(first if e == 0 else ~first, gp.astype(F32), 0.0).astype(BF16)
                total += dot(own, xp, 1, 1) * decay
                found.append((dot(weighted, xp), dot(weighted, gp, 0, 0)))
            within_ref[:, span] = jnp.where(first, found[0][0], found[1][0])
            dxw_ref[:, span] = jnp.where(first, found[0][1], found[1][1])
        halved = total.astype(BF16)
        grads[0] = dot(b, halved, 0, 1)
        grads[1] = dot(c, halved, 0, 0)

    second = lax.rem(head, 2) == 1

    @pl.when(~second)
    def _():
        attend()

    @pl.when(outer)
    def _():
        pl.semaphore_wait(barrier, 2 * groups + peers - 1)

    @pl.when(~outer)
    def _():
        pl.semaphore_wait(barrier, 2 * groups + 1 + peers - 1)

    @pl.when(second)
    def _():
        attend()

    def up_copy(scan, ch, source, to):
        return pltpu.make_async_remote_copy(
            src_ref=source, dst_ref=up_in.at[scan, ch], send_sem=up_send.at[scan, ch],
            recv_sem=up_recv.at[scan, ch], device_id=to, device_id_type=MESH,
        )

    def gain_copy(scan, source, to):
        return pltpu.make_async_remote_copy(
            src_ref=source, dst_ref=gain_in.at[scan], send_sem=gain_send.at[scan],
            recv_sem=gain_recv.at[scan], device_id=to, device_id_type=MESH,
        )

    def down_copy(scan, ch, to):
        return pltpu.make_async_remote_copy(
            src_ref=down_out.at[scan, ch], dst_ref=down_in.at[scan, ch], send_sem=down_send.at[scan, ch],
            recv_sem=down_recv.at[scan, ch], device_id=to, device_id_type=MESH,
        )

    rank = jnp.where(late == 0, group, groups - 1 - group)

    def owner_copy(ch):
        return pltpu.make_async_remote_copy(
            src_ref=up_out.at[late, ch], dst_ref=at_owner.at[rank], send_sem=rep_send.at[ch],
            recv_sem=own_recv.at[rank], device_id=owner(late, ch), device_id_type=MESH,
        )

    def gain_far_copy(ch):
        return pltpu.make_async_remote_copy(
            src_ref=gain_out.at[late], dst_ref=gain_at.at[rank], send_sem=gain_far_send.at[ch],
            recv_sem=gain_far_recv.at[rank], device_id=owner(late, ch), device_id_type=MESH,
        )

    def arrived(buffer, sem, k):
        pltpu.make_async_remote_copy(
            src_ref=buffer.at[k], dst_ref=buffer.at[k], send_sem=own_send.at[k],
            recv_sem=sem.at[k], device_id=e_to, device_id_type=MESH,
        ).wait_recv()

    def back_copy(k):
        to = jnp.where(scan_owned == 0, k * GROUP, (groups - 1 - k) * GROUP + GROUP - 1)
        return pltpu.make_async_remote_copy(
            src_ref=from_owner.at[k], dst_ref=down_in.at[scan_owned, mine], send_sem=own_send.at[k],
            recv_sem=down_recv.at[scan_owned, mine], device_id=(to, head), device_id_type=MESH,
        )

    def unit_copy(u):
        return pltpu.make_async_remote_copy(
            src_ref=unit_out.at[u], dst_ref=unit_in.at[head], send_sem=unit_send.at[u],
            recv_sem=unit_recv.at[head], device_id=(seq, u), device_id_type=MESH,
        )

    def unit_from(u):
        return pltpu.make_async_remote_copy(
            src_ref=unit_in.at[u], dst_ref=unit_in.at[u], send_sem=unit_send.at[u],
            recv_sem=unit_recv.at[u], device_id=(seq, u), device_id_type=MESH,
        )

    final = late * parts + parts - 1

    def last_copy(u):
        return pltpu.make_async_remote_copy(
            src_ref=unit_out.at[final], dst_ref=last_in.at[head], send_sem=last_send.at[u],
            recv_sem=last_recv.at[head], device_id=(seq, u), device_id_type=MESH,
        )

    def last_from(u):
        return pltpu.make_async_remote_copy(
            src_ref=last_in.at[u], dst_ref=last_in.at[u], send_sem=last_send.at[u],
            recv_sem=last_recv.at[u], device_id=(seq, u), device_id_type=MESH,
        )

    def full_copy(u):
        return pltpu.make_async_remote_copy(
            src_ref=full.at[head], dst_ref=full.at[head], send_sem=full_send.at[u],
            recv_sem=full_recv.at[head], device_id=(seq, u), device_id_type=MESH,
        )

    def full_from(u):
        return pltpu.make_async_remote_copy(
            src_ref=full.at[u], dst_ref=full.at[u], send_sem=full_send.at[u],
            recv_sem=full_recv.at[u], device_id=(seq, u), device_id_type=MESH,
        )

    def rise(scan, ch):
        up_copy(scan, ch, up_out.at[scan, ch], e_to).wait_recv()
        up_out[scan, ch] = own_in[scan, ch] + gain * up_in[scan, ch]

    def gain_rise(scan):
        gain_copy(scan, gain_own, e_to).wait_recv()
        gain_out[scan] = gain_own[...] * gain_in[scan]

    @pl.when(outer)
    def _():
        gain_copy(early, gain_own, e_to).start()

        def send(ch, _):
            up_copy(early, ch, own_in.at[early, ch], e_to).start()
            return 0

        lax.fori_loop(0, chunks, send, 0)
        gain_rise(late)

        def tell(ch, _):
            @pl.when(rank < groups - 1)
            def _():
                gain_far_copy(ch).start()

            return 0

        lax.fori_loop(0, chunks, tell, 0)

        def finish(ch, _):
            rise(late, ch)

            @pl.when(rank < groups - 1)
            def _():
                owner_copy(ch).start()

            return 0

        lax.fori_loop(0, chunks, finish, 0)

    lag = jnp.where(second, min(5, chunks), min(7, chunks))

    @pl.when(~outer)
    def _():
        gain_rise(early)
        gain_copy(early, gain_out.at[early], e_to).start()

        def step(i, _):
            @pl.when(i < chunks)
            def _():
                rise(early, i)
                up_copy(early, i, up_out.at[early, i], e_to).start()

            @pl.when(i == lag)
            def _():
                gain_rise(late)
                gain_copy(late, gain_out.at[late], l_to).start()

            @pl.when(i >= lag)
            def _():
                rise(late, i - lag)
                up_copy(late, i - lag, up_out.at[late, i - lag], l_to).start()

            return 0

        lax.fori_loop(0, chunks + lag, step, 0)

        def told(k, _):
            arrived(gain_at, gain_far_recv, k)
            return 0

        lax.fori_loop(0, groups - 1, told, 0)
        gain_at[groups - 1] = jnp.zeros((1, PAIR), F32)
        gains = jnp.concatenate([gain_at[k] for k in range(groups)], axis=0)
        r = lax.broadcasted_iota(jnp.int32, (PAIR, lanes), 0)
        l = lax.broadcasted_iota(jnp.int32, (PAIR, lanes), 1)
        gain_wide[...] = split_dot(gains, jnp.where(l // HEADDIM == r, 1.0, 0.0).astype(BF16))
        arrived(at_owner, own_recv, 0)

        def hand_out(k, entering):
            from_owner[k] = entering
            back_copy(k).start()

            @pl.when(k < groups - 1)
            def _():
                arrived(at_owner, own_recv, k)

            return gain_wide[pl.ds(k, 1)] * entering + at_owner[k]

        at_owner[groups - 1] = jnp.zeros((deep, lanes), F32)
        lax.fori_loop(1, groups, hand_out, at_owner[0])

    def landed(scan, ch):
        down_copy(scan, ch, e_to).wait_recv()

    begins = jnp.where(early == 0, group, groups - 1 - group) == 0

    def fall(scan, ch, to):
        down_out[scan, ch] = own_in[scan, ch] + gain * down_in[scan, ch]
        down_copy(scan, ch, to).start()

    def unit(scan, ch):
        @pl.when(lax.rem(ch + 1, per) == 0)
        def _():
            q = ch // per
            u = scan * parts + q
            state = down_in[scan, pl.ds(q * per, per)].reshape(wide, lanes).astype(BF16)
            part = grads[scan, pl.ds(pl.multiple_of(q * wide, wide), wide)]
            unit_out[u] = part + dot(state, factor[scan], 1, 1)

            @pl.when((u != head) & (u != final))
            def _():
                unit_copy(u).start()

            @pl.when(u == final)
            def _():
                for o in range(1, peers):
                    last_copy(lax.rem(head + o, peers)).start()

    @pl.when(outer)
    def _():
        def one(i, _):
            @pl.when(begins)
            def _():
                down_in[early, i] = jnp.zeros((deep, lanes), F32)

            @pl.when(~begins)
            def _():
                landed(early, i)

            fall(early, i, e_to)
            return 0

        lax.fori_loop(0, chunks, one, 0)

        def add(i, _):
            unit(early, i)
            return 0

        lax.fori_loop(0, chunks, add, 0)

        def two(i, _):
            landed(late, i)
            unit(late, i)
            return 0

        lax.fori_loop(0, chunks, two, 0)

    @pl.when(~outer)
    def _():
        def step(i, _):
            @pl.when(i < chunks)
            def _():
                landed(early, i)
                fall(early, i, e_to)

            @pl.when(i >= lag)
            def _():
                landed(late, i - lag)
                fall(late, i - lag, l_to)

            @pl.when(i < chunks)
            def _():
                unit(early, i)

            @pl.when(i >= lag)
            def _():
                unit(late, i - lag)

            return 0

        lax.fori_loop(0, chunks + lag, step, 0)

    spread = lane_head(lanes, heads)
    rising = jnp.zeros((tokens, heads), F32)
    falling = jnp.zeros((tokens, heads), F32)
    start = down_in[0].reshape(STATE, lanes)
    adj = down_in[1].reshape(STATE, lanes)
    @pl.when(head != final)
    def _():
        def add(o, total):
            u = lax.rem(head + o, peers)
            unit_from(u).wait_recv()
            return total + unit_in[u]

        full[head] = lax.fori_loop(1, peers, add, unit_out[head])
        for o in range(1, peers):
            full_copy(lax.rem(head + o, peers)).start()

    for j in range(pairs):
        span = slice(j * PAIR, (j + 1) * PAIR)
        x, g = x_ref[:, span].astype(F32), g_ref[:, span].astype(F32)
        own = spread[span]
        out = within_ref[:, span] + grown_ref[:, span] * dot(c, start[:, span].astype(BF16))
        pushed = left_ref[:, span] * dot(b, adj[:, span].astype(BF16))
        out_ref[:, span] = out.astype(BF16)
        dx_ref[:, span] = (dxw_ref[:, span] + pushed).astype(BF16)
        rising += split_dot(g * out - x * dxw_ref[:, span], own)
        falling += split_dot(x * pushed, own)

    meet = jnp.sum(start * adj, axis=0, keepdims=True) * gain
    meet = jnp.broadcast_to(meet, (8, lanes))
    high = meet.astype(BF16)
    low = (meet - high.astype(F32)).astype(BF16)
    where = head_of_lane(heads, lanes)
    last = dot(where, high, 1, 1) + dot(where, low, 1, 1)
    dldt_ref[...] = (
        dot(rising, lower(tokens).astype(F32), 0, 0, precision=HIGHEST)
        + dot(falling, lower(tokens, True).astype(F32), 0, 1, precision=HIGHEST)
        + last[:, :1]
    )

    gain_copy(early, gain_own, e_to).wait_send()

    def gone(ch, _):
        up_copy(early, ch, up_out.at[early, ch], e_to).wait_send()
        down_copy(early, ch, e_to).wait_send()

        @pl.when(outer)
        def _():
            @pl.when(rank < groups - 1)
            def _():
                owner_copy(ch).wait_send()
                gain_far_copy(ch).wait_send()

        @pl.when(~outer)
        def _():
            up_copy(late, ch, up_out.at[late, ch], l_to).wait_send()
            down_copy(late, ch, l_to).wait_send()

            @pl.when(ch > 0)
            def _():
                back_copy(ch).wait_send()

        return 0

    lax.fori_loop(0, chunks, gone, 0)

    @pl.when(~outer)
    def _():
        gain_copy(late, gain_own, l_to).wait_send()

    last_in[head] = unit_out[final]
    for o in range(1, peers):
        u = lax.rem(head + o, peers)
        last_copy(u).wait_send()
        last_from(u).wait_recv()

        @pl.when(u != final)
        def _():
            unit_copy(u).wait_send()
            full_from(u).wait_recv()

        @pl.when(head != final)
        def _():
            full_copy(u).wait_send()

    total = last_in[0]
    for u in range(1, peers):
        total += last_in[u]
    full[final] = total
    gc_ref[...] = full[:parts].reshape(STATE, tokens).T
    gb_ref[...] = full[parts:].reshape(STATE, tokens).T


def store_kernel(*refs):
    sems = refs[-1]
    copies = [pltpu.make_async_copy(refs[i], refs[5 + i], sems.at[i]) for i in range(5)]
    for copy in copies:
        copy.start()
    for copy in copies:
        copy.wait()


def shards(inputs, log_decay, b_proj, c_proj, grad_out):
    tokens, heads = log_decay.shape
    lanes = heads * HEADDIM
    groups = lax.axis_size("seq") // GROUP
    peers = lax.axis_size("head")
    deep = STATE // groups
    unit = (peers, STATE // (peers // 2), tokens)
    chunk = (2, groups, deep, lanes)
    dma = pltpu.SemaphoreType.DMA
    half = jax.ShapeDtypeStruct(inputs.shape, BF16)
    thin = jax.ShapeDtypeStruct((tokens, STATE), F32)
    whole = pl.BlockSpec(memory_space=VMEM)
    results = (half, half, jax.ShapeDtypeStruct((heads, tokens), F32), thin, thin)
    held = pl.pallas_call(
        main_kernel,
        out_shape=tuple(pltpu.VMEM(a.shape, a.dtype) for a in results),
        in_specs=[pl.BlockSpec(memory_space=pl.ANY)] * 5,
        out_specs=(whole,) * 5,
        scratch_shapes=[
            pltpu.VMEM((tokens, lanes), BF16), pltpu.VMEM((heads, tokens), F32),
            pltpu.VMEM((tokens, STATE), BF16), pltpu.VMEM((tokens, STATE), BF16),
            pltpu.VMEM((tokens, lanes), BF16), dma((5,)),
            pltpu.VMEM((tokens, lanes), F32), pltpu.VMEM((tokens, lanes), F32),
            pltpu.VMEM((tokens, lanes), F32), pltpu.VMEM((tokens, lanes), F32),
            pltpu.VMEM((2, tokens, lanes), BF16), pltpu.VMEM((2, STATE, tokens), F32),
            pltpu.VMEM(chunk, F32), pltpu.VMEM(chunk, F32), pltpu.VMEM(chunk, F32),
            pltpu.VMEM(chunk, F32), pltpu.VMEM(chunk, F32),
            pltpu.VMEM((groups, deep, lanes), F32), pltpu.VMEM((groups, deep, lanes), F32),
            pltpu.VMEM((1, PAIR), F32), pltpu.VMEM((2, 1, PAIR), F32), pltpu.VMEM((2, 1, PAIR), F32),
            pltpu.VMEM((groups, 1, PAIR), F32), pltpu.VMEM((groups, lanes), F32),
            pltpu.VMEM(unit, F32), pltpu.VMEM(unit, F32), pltpu.VMEM(unit, F32), pltpu.VMEM(unit, F32),
            dma((2, groups)), dma((2, groups)), dma((groups,)), dma((groups,)),
            dma((2, groups)), dma((2, groups)), dma((groups,)),
            dma((2,)), dma((2,)), dma((groups,)), dma((groups,)),
            dma((peers,)), dma((peers,)), dma((peers,)), dma((peers,)), dma((peers,)), dma((peers,)),
        ],
        compiler_params=pltpu.CompilerParams(
            collective_id=0, has_side_effects=True, vmem_limit_bytes=56 * 2**20
        ),
        name="scan",
    )(inputs, log_decay.T, b_proj, c_proj, grad_out)
    outputs, grad_inputs, grad_decay, grad_b, grad_c = pl.pallas_call(
        store_kernel,
        out_shape=results,
        in_specs=[pl.BlockSpec(memory_space=pl.ANY)] * 5,
        out_specs=(pl.BlockSpec(memory_space=pl.ANY),) * 5,
        scratch_shapes=[dma((5,))],
        name="store",
    )(*(pltpu.with_memory_space_constraint(array, VMEM) for array in held))
    return outputs, grad_inputs, grad_decay.T, grad_b, grad_c


def solution(mesh):
    placed = (P("seq", "head"), P("seq", "head"), P("seq", None), P("seq", None), P("seq", "head"))
    return jax.shard_map(
        shards,
        mesh=mesh,
        in_specs=placed,
        out_specs=(
            P("seq", "head"),
            P("seq", "head"),
            P("seq", "head"),
            P("seq", None),
            P("seq", None),
        ),
        check_vma=False,
    )
```
